32 devices in a mesh: dp: 4 (over y, x), seq: 8 (over z, core).
Axes of the slice: x: 2, y: 2, z: 4, core: 2. Of those that a mesh axis runs over, the one named last changes fastest.
Arguments:
- query_gate: bfloat16 [4, 1024, 4096], P('dp', 'seq'), may hold values from -6 to 6
- key_gate: bfloat16 [4, 1024, 4096], P('dp', 'seq'), may hold values from -6 to 6
- value_feat: bfloat16 [4, 1024, 4096], P('dp', 'seq'), may hold values from -6 to 6
- filters: bfloat16 [256, 128], replicated, may hold values from -0.5 to 0.5
- grad_out: bfloat16 [4, 1024, 4096], P('dp', 'seq'), may hold values from -6 to 6
- basis_prev: float32 [128, 16], replicated, may hold values from -6 to 6
Outputs:
- mixed_out: bfloat16 [4, 1024, 4096], P('dp', 'seq')
- grad_query: bfloat16 [4, 1024, 4096], P('dp', 'seq')
- grad_key: bfloat16 [4, 1024, 4096], P('dp', 'seq')
- grad_value: bfloat16 [4, 1024, 4096], P('dp', 'seq')
- low_rank_grad: float32 [256, 128], replicated
- basis_next: float32 [128, 16], replicated
The draws below stay inside these ranges and needn't reach their ends.
All inputs are finite; a program needn't handle non-finite values.
Results may differ from the reference program's by a relative error of at most 0.0061.
Values may be sent and summed in bfloat16 or wider, within the bound.
A program may use at most 192 MiB of HBM per device.

```python
import jax
import jax.numpy as jnp
from jax import lax

CHANNELS = 4096
GROUP = 16
TAPS = 128
RANK = 16
GROUPS = 256
BATCH = 4
SEQ_LEN = 1024


def shard_levels(stream_key, dims, shards, smallest, largest):
    loudness = 1.0
    for position, shards_of in shards:
        heights = jax.random.uniform(jax.random.fold_in(jax.random.fold_in(stream_key, 6), position), (shards_of,), jnp.float32, smallest / len(shards), largest / len(shards))
        loudness = loudness * jnp.repeat(jnp.exp(heights), dims[position] // shards_of).reshape((-1,) + (1,) * (len(dims) - 1 - position))
    return loudness


def bell_draw(stream_key, extent, deviation, bound, shards=(), kind=jnp.bfloat16):
    values = jax.random.normal(stream_key, extent, jnp.float32) * deviation
    if len(shards) > 0:
        values = shard_levels(stream_key, extent, shards, -0.22, 0.18) * values
    return jnp.clip(values, min=-bound, max=bound).astype(kind)


def setup_inputs(seed: int = 0) -> dict:
    streams_of = jax.random.split(jax.random.key(seed), 7)
    return {
        "query_gate": bell_draw(streams_of[0], (BATCH, SEQ_LEN, CHANNELS), 1.0, 6.0, ((0, 4), (1, 8))),
        "key_gate": bell_draw(streams_of[1], (BATCH, SEQ_LEN, CHANNELS), 1.0, 6.0, ((0, 4), (1, 8))),
        "value_feat": bell_draw(streams_of[2], (BATCH, SEQ_LEN, CHANNELS), 1.0, 6.0, ((0, 4), (1, 8))),
        "filters": bell_draw(streams_of[3], (GROUPS, TAPS), TAPS ** -0.5, 0.5),
        "grad_out": bell_draw(streams_of[4], (BATCH, SEQ_LEN, CHANNELS), 1.0, 6.0, ((0, 4), (1, 8))),
        "basis_prev": bell_draw(streams_of[5], (TAPS, RANK), 1.0, 6.0, (), jnp.float32),
    }


def orthonormal(left):
    columns = []
    for index in range(left.shape[1]):
        column = left[:, index]
        if index > 0:
            basis = jnp.stack(columns, axis=1)
            coeffs = jnp.dot(basis.T, column, precision=lax.Precision.HIGHEST)
            column = column - jnp.dot(basis, coeffs, precision=lax.Precision.HIGHEST)
        columns.append(column / jnp.sqrt(jnp.sum(column * column) + 1e-06))
    return jnp.stack(columns, axis=1)

def reference(query_gate, key_gate, value_feat, filters, grad_out, basis_prev):
    product = (key_gate.astype(jnp.float32) * value_feat.astype(jnp.float32)).astype(jnp.bfloat16)
    grad_conv = (grad_out.astype(jnp.float32) * query_gate.astype(jnp.float32)).astype(jnp.bfloat16)
    length = SEQ_LEN + TAPS
    width_blk = min(256, CHANNELS)
    count = CHANNELS // width_blk
    per_chan = jnp.repeat(filters.astype(jnp.float32), GROUP, axis=0)

    def one_block(index):
        start = index * width_blk
        piece_s = lax.dynamic_slice_in_dim(product, start, width_blk, 2).astype(jnp.float32)
        piece_d = lax.dynamic_slice_in_dim(grad_conv, start, width_blk, 2).astype(jnp.float32)
        piece_h = lax.dynamic_slice_in_dim(per_chan, start, width_blk, 0)
        spec_s = jnp.fft.rfft(piece_s, length, axis=1)
        spec_d = jnp.fft.rfft(piece_d, length, axis=1)
        spec_h = jnp.fft.rfft(piece_h.T, length, axis=0)[None]
        conv_b = jnp.fft.irfft(spec_s * spec_h, length, axis=1)[:, :SEQ_LEN]
        back_b = jnp.fft.irfft(spec_d * jnp.conj(spec_h), length, axis=1)[:, :SEQ_LEN]
        cross = jnp.fft.irfft(spec_d * jnp.conj(spec_s), length, axis=1)[:, :TAPS]
        cross = lax.optimization_barrier(jnp.sum(cross, axis=0)).reshape(TAPS, width_blk // GROUP, GROUP).sum(axis=2)
        return (conv_b.astype(jnp.float32), back_b.astype(jnp.float32), cross.T.astype(jnp.float32))
    conv_all, back_all, grad_rows = lax.map(one_block, jnp.arange(count, dtype=jnp.int32))
    conv = jnp.moveaxis(conv_all, 0, 2).reshape(BATCH, SEQ_LEN, CHANNELS)
    grad_product = jnp.moveaxis(back_all, 0, 2).reshape(BATCH, SEQ_LEN, CHANNELS)
    grad_filter = grad_rows.reshape(GROUPS, TAPS)
    mixed_out = (query_gate.astype(jnp.float32) * conv).astype(jnp.bfloat16)
    grad_query = (grad_out.astype(jnp.float32) * conv).astype(jnp.bfloat16)
    grad_key = (grad_product * value_feat.astype(jnp.float32)).astype(jnp.bfloat16)
    grad_value = (grad_product * key_gate.astype(jnp.float32)).astype(jnp.bfloat16)
    left = jnp.dot(grad_filter, basis_prev, precision=lax.Precision.HIGHEST)
    ortho = orthonormal(left)
    scale = (BATCH * SEQ_LEN * GROUP) ** (-0.5)
    basis_next = jnp.dot(grad_filter.T, ortho, precision=lax.Precision.HIGHEST) * scale
    low_rank_grad = jnp.dot(ortho, basis_next.T, precision=lax.Precision.HIGHEST)
    return (mixed_out, grad_query, grad_key, grad_value, low_rank_grad, basis_next)
```

```python
import functools

import jax
import jax.numpy as jnp
from jax import lax
from jax.experimental import pallas as pl
from jax.experimental.pallas import tpu as pltpu
from jax.sharding import PartitionSpec as P

MESH = pl.DeviceIdType.MESH
HIGHEST = lax.Precision.HIGHEST
F32 = jnp.float32
BF16 = jnp.bfloat16
STEP = 32
LANES = 128


def flipped(size, dtype):
    rows = lax.broadcasted_iota(jnp.int32, (size, size), 0)
    cols = lax.broadcasted_iota(jnp.int32, (size, size), 1)
    return jnp.where(rows + cols == size - 1, 1.0, 0.0).astype(dtype)


def gated(left, right):
    return (left.astype(F32) * right.astype(F32)).astype(BF16)


def halo_kernel(chunks, q, k, v, g, prod_halo, grad_halo, prod, grad, send_p, recv_p, send_g, recv_g):
    me = lax.axis_index("seq")
    last = lax.axis_size("seq") - 1
    tok, channels = q.shape
    width = channels // chunks

    barrier = pltpu.get_barrier_semaphore()

    @pl.when(me > 0)
    def _():
        pl.semaphore_signal(barrier, inc=1, device_id={"seq": me - 1}, device_id_type=MESH)

    @pl.when(me < last)
    def _():
        pl.semaphore_signal(barrier, inc=1, device_id={"seq": me + 1}, device_id_type=MESH)

    def to_next(c):
        lanes = pl.ds(c * width, width)
        return pltpu.make_async_remote_copy(
            src_ref=prod.at[:, lanes], dst_ref=prod_halo.at[:, lanes], send_sem=send_p.at[c],
            recv_sem=recv_p.at[c], device_id={"seq": me + 1}, device_id_type=MESH)

    def to_previous(c):
        lanes = pl.ds(c * width, width)
        return pltpu.make_async_remote_copy(
            src_ref=grad.at[:, lanes], dst_ref=grad_halo.at[:, lanes], send_sem=send_g.at[c],
            recv_sem=recv_g.at[c], device_id={"seq": me - 1}, device_id_type=MESH)

    flip = flipped(tok, BF16)
    for c in range(chunks):
        lanes = pl.ds(c * width, width)
        prod[:, lanes] = gated(k[:, lanes], v[:, lanes])
        grad[:, lanes] = jnp.dot(
            flip, gated(g[:, lanes], q[:, lanes]), preferred_element_type=F32).astype(BF16)
        if c == 0:
            pl.semaphore_wait(barrier, (me > 0).astype(jnp.int32) + (me < last).astype(jnp.int32))

        @pl.when(me < last)
        def _():
            to_next(c).start()

        @pl.when(me > 0)
        def _():
            to_previous(c).start()

    for c in range(chunks):
        @pl.when(me < last)
        def _():
            to_next(c).wait_send()
            to_previous(c).wait_recv()

        @pl.when(me > 0)
        def _():
            to_previous(c).wait_send()
            to_next(c).wait_recv()


def mixer_kernel(group, q, k, v, g, prod_halo, grad_halo, lines, mixed, grad_q, grad_k, grad_v, lag, ext):
    me = lax.axis_index("seq")
    last = lax.axis_size("seq") - 1
    tok, width = q.shape
    subs = width // LANES
    per = LANES // group
    blocks = tok // STEP
    rows = 2 * tok
    flip = flipped(tok, BF16)
    prod = gated(k[...], v[...])
    grad = jnp.dot(flip, gated(g[...], q[...]), preferred_element_type=F32).astype(BF16)
    before = jnp.where(me > 0, prod_halo[...], jnp.zeros_like(prod))
    after = jnp.where(me < last, grad_halo[...], jnp.zeros_like(grad))
    for s in range(subs):
        lanes = slice(s * LANES, (s + 1) * LANES)
        low = slice(2 * s * LANES, (2 * s + 1) * LANES)
        high = slice((2 * s + 1) * LANES, (2 * s + 2) * LANES)
        ext[0:tok, low] = before[:, lanes]
        ext[tok:rows, low] = prod[:, lanes]
        ext[0:tok, high] = after[:, lanes]
        ext[tok:rows, high] = grad[:, lanes]
    ext[rows:, :] = jnp.zeros((ext.shape[0] - rows, ext.shape[1]), BF16)
    owner = lax.broadcasted_iota(jnp.int32, (STEP, 2 * LANES), 1) % LANES // group
    flip2 = jnp.concatenate([flip, flip], axis=1)
    for s in range(subs):
        lanes = slice(s * LANES, (s + 1) * LANES)
        low = slice(2 * s * LANES, (2 * s + 1) * LANES)
        high = slice((2 * s + 1) * LANES, (2 * s + 2) * LANES)
        both = slice(2 * s * LANES, (2 * s + 2) * LANES)
        band = jnp.concatenate(
            [
                pltpu.roll(
                    jnp.broadcast_to(lines[s * per + i : s * per + i + 1, :], (STEP, rows)),
                    0, axis=1, stride=1, stride_axis=0,
                ).astype(BF16)
                for i in range(per)
            ],
            axis=0,
        )
        cross = jnp.zeros((per * STEP, rows), F32)
        for pair in range(0, blocks, 2):
            one, two = pair, pair + 1
            at_one = tok + STEP * (blocks - 1 - one)
            at_two = tok + STEP * (blocks - 1 - two)
            cot = jnp.concatenate([ext[at_one : at_one + STEP, high], ext[at_two : at_two + STEP, high]], axis=1)
            windows = jnp.concatenate(
                [ext[STEP * one : STEP * one + rows, low], ext[STEP * two : STEP * two + rows, low]], axis=1)
            masked = jnp.concatenate(
                [jnp.where(owner == i, cot, jnp.zeros_like(cot)) for i in range(per)], axis=0)
            cross = cross + lax.dot_general(
                masked, windows, (((1,), (1,)), ((), ())), preferred_element_type=F32)
        sums = []
        for i in range(per):
            skewed = pltpu.roll(
                cross[i * STEP : (i + 1) * STEP, :], rows - STEP, axis=1, stride=1, stride_axis=0)
            sums.append(jnp.sum(skewed, axis=0, keepdims=True)[:, :tok])
        lag[s * per : (s + 1) * per, :] = jnp.concatenate(sums, axis=0)
        parts = []
        for a in range(blocks):
            res = jnp.dot(band, ext[STEP * a : STEP * a + rows, both], preferred_element_type=F32)
            out = res[0:STEP, :]
            for i in range(1, per):
                out = jnp.where(owner == i, res[i * STEP : (i + 1) * STEP, :], out)
            parts.append(out)
        whole = jnp.concatenate(parts, axis=0)
        conv = whole[:, :LANES]
        back = whole[:, LANES:]
        coarse = back.astype(BF16)
        fine = (back - coarse.astype(F32)).astype(BF16)
        grad_prod = jnp.dot(flip2, jnp.concatenate([coarse, fine], axis=0), preferred_element_type=F32)
        mixed[:, lanes] = (q[:, lanes].astype(F32) * conv).astype(BF16)
        grad_q[:, lanes] = (g[:, lanes].astype(F32) * conv).astype(BF16)
        grad_k[:, lanes] = (grad_prod * v[:, lanes].astype(F32)).astype(BF16)
        grad_v[:, lanes] = (grad_prod * k[:, lanes].astype(F32)).astype(BF16)


def factor_kernel(scale, lag, basis, low_rank, basis_next, parts, mine, gathered, send_a, recv_a, send_b, recv_b):
    dp, seq = lax.axis_size("dp"), lax.axis_size("seq")
    count = dp * seq
    me = lax.axis_index("dp") * seq + lax.axis_index("seq")
    rows = lag.shape[1]

    def where(k):
        peer = lax.rem(me + k, count)
        return peer, (peer // seq, lax.rem(peer, seq))

    barrier = pltpu.get_barrier_semaphore()

    @pl.loop(1, count)
    def _(k):
        pl.semaphore_signal(barrier, inc=1, device_id=where(k)[1], device_id_type=MESH)

    pl.semaphore_wait(barrier, count - 1)

    def scatter(k):
        peer, place = where(k)
        return pltpu.make_async_remote_copy(
            src_ref=lag.at[peer], dst_ref=parts.at[k], send_sem=send_a.at[k],
            recv_sem=recv_a.at[k], device_id=place, device_id_type=MESH)

    def gather(k):
        peer, place = where(k)
        return pltpu.make_async_remote_copy(
            src_ref=mine, dst_ref=gathered.at[me], send_sem=send_b.at[k],
            recv_sem=recv_b.at[k], device_id=place, device_id_type=MESH)

    @pl.loop(1, count)
    def _(k):
        scatter(k).start()

    parts[0] = lag[me]

    @pl.loop(1, count)
    def _(k):
        scatter(k).wait_recv()

    mine[...] = jnp.sum(parts[...], axis=0)

    @pl.loop(1, count)
    def _(k):
        gather(k).start()

    gathered[me] = mine[...]

    @pl.loop(1, count)
    def _(k):
        peer = lax.rem(me + count - k, count)
        pltpu.make_async_remote_copy(
            src_ref=mine, dst_ref=gathered.at[peer], send_sem=send_b.at[k],
            recv_sem=recv_b.at[k], device_id=where(k)[1], device_id_type=MESH).wait_recv()

    grads = gathered[...].reshape(count * rows, lag.shape[2])
    contract = (((1,), (1,)), ((), ()))
    left = lax.dot_general(basis[...], grads, contract, precision=HIGHEST, preferred_element_type=F32)
    rank = left.shape[0]
    index = lax.broadcasted_iota(jnp.int32, left.shape, 0)
    rest = left
    ortho = jnp.zeros_like(left)
    for i in range(rank):
        column = rest[i : i + 1, :]
        norm = jnp.sum(column * column, axis=1, keepdims=True) + 1e-06
        along = jnp.sum(left * column, axis=1, keepdims=True)
        ortho = jnp.where(index == i, column / jnp.sqrt(norm), ortho)
        rest = rest - (along / norm) * column
    right = jnp.dot(ortho, grads, precision=HIGHEST, preferred_element_type=F32) * scale
    flip = flipped(lag.shape[2], F32)
    basis_next[...] = lax.dot_general(flip, right, contract, precision=HIGHEST, preferred_element_type=F32)
    right = jnp.dot(right, flip, precision=HIGHEST, preferred_element_type=F32)
    low_rank[...] = lax.dot_general(
        ortho, right, (((0,), (0,)), ((), ())), precision=HIGHEST, preferred_element_type=F32)

    @pl.loop(1, count)
    def _(k):
        scatter(k).wait_send()
        gather(k).wait_send()


def on_device(query_gate, key_gate, value_feat, filters, grad_out, basis_prev):
    q, k, v, g = query_gate[0], key_gate[0], value_feat[0], grad_out[0]
    tok, channels = q.shape
    groups, taps = filters.shape
    group = channels // groups
    count = lax.axis_size("dp") * lax.axis_size("seq")
    rank = basis_prev.shape[1]
    vmem = pl.BlockSpec(memory_space=pltpu.VMEM)
    anywhere = pl.BlockSpec(memory_space=pl.ANY)
    block = jax.ShapeDtypeStruct((tok, channels), BF16)

    chunks = 8
    prod_halo, grad_halo = pl.pallas_call(
        functools.partial(halo_kernel, chunks),
        out_shape=(block, block),
        in_specs=[vmem] * 4,
        out_specs=(anywhere, anywhere),
        scratch_shapes=[pltpu.VMEM((tok, channels), BF16)] * 2 + [pltpu.SemaphoreType.DMA((chunks,))] * 4,
        compiler_params=pltpu.CompilerParams(
            collective_id=0, has_side_effects=True, vmem_limit_bytes=48 * 2**20),
        name="halo",
    )(q, k, v, g)

    line = jnp.pad(filters[:, ::-1].astype(F32), ((0, 0), (1, 2 * tok - taps - 1)))
    width = 512
    wide = pl.BlockSpec((tok, width), lambda i: (0, i))
    mixed, grad_q, grad_k, grad_v, lag = pl.pallas_call(
        functools.partial(mixer_kernel, group),
        grid=(channels // width,),
        out_shape=(block,) * 4 + (jax.ShapeDtypeStruct((groups, taps), F32),),
        in_specs=[wide] * 6 + [pl.BlockSpec((width // group, 2 * tok), lambda i: (i, 0))],
        out_specs=[wide] * 4 + [pl.BlockSpec((width // group, taps), lambda i: (i, 0))],
        scratch_shapes=[pltpu.VMEM((3 * tok - STEP, 2 * width), BF16)],
        compiler_params=pltpu.CompilerParams(vmem_limit_bytes=48 * 2**20),
        name="mixer",
    )(q, k, v, g, prod_halo, grad_halo, line)

    scale = (lax.axis_size("dp") * lax.axis_size("seq") * tok * group) ** (-0.5)
    rows = groups // count
    low_rank, basis_next = pl.pallas_call(
        functools.partial(factor_kernel, scale),
        out_shape=(
            jax.ShapeDtypeStruct((groups, taps), F32),
            jax.ShapeDtypeStruct((taps, rank), F32),
        ),
        in_specs=[vmem] * 2,
        out_specs=(vmem, vmem),
        scratch_shapes=[
            pltpu.VMEM((count, rows, taps), F32),
            pltpu.VMEM((rows, taps), F32),
            pltpu.VMEM((count, rows, taps), F32),
        ] + [pltpu.SemaphoreType.DMA((count,))] * 4,
        compiler_params=pltpu.CompilerParams(
            collective_id=1, has_side_effects=True, vmem_limit_bytes=16 * 2**20),
        name="factors",
    )(lag.reshape(count, rows, taps), basis_prev[::-1].T)
    return (mixed[None], grad_q[None], grad_k[None], grad_v[None], low_rank, basis_next)


def solution(mesh):
    spec = P("dp", "seq", None)
    return jax.shard_map(
        on_device,
        mesh=mesh,
        in_specs=(spec, spec, spec, P(), spec, P()),
        out_specs=(spec, spec, spec, spec, P(), P()),
        check_vma=False,
    )
```

```python
import functools

import jax
import jax.numpy as jnp
from jax import lax
from jax.experimental import pallas as pl
from jax.experimental.pallas import tpu as pltpu
from jax.sharding import PartitionSpec as P

MESH = pl.DeviceIdType.MESH
HIGHEST = lax.Precision.HIGHEST
F32 = jnp.float32
BF16 = jnp.bfloat16
STEP = 32
LANES = 128
CHUNKS = 8
NT = (((1,), (1,)), ((), ()))
TN = (((0,), (0,)), ((), ()))


def flipped(size, dtype):
    rows = lax.broadcasted_iota(jnp.int32, (size, size), 0)
    cols = lax.broadcasted_iota(jnp.int32, (size, size), 1)
    return jnp.where(rows + cols == size - 1, 1.0, 0.0).astype(dtype)


def gated(left, right):
    return (left.astype(F32) * right.astype(F32)).astype(BF16)


def mixer_kernel(
    scale, q_in, k_in, v_in, g_in, filters, basis,
    mixed_out, grad_q_out, grad_k_out, grad_v_out, low_rank, basis_next,
    q, k, v, g, mixed, grad_q, grad_k, grad_v, ext_p, ext_g, bands, lag, parts, mine, gathered,
    load, store, send_p, recv_p, send_g, recv_g, send_a, recv_a, send_b, recv_b,
):
    dp, seq = lax.axis_size("dp"), lax.axis_size("seq")
    count = dp * seq
    pos = lax.axis_index("seq")
    last = seq - 1
    me = lax.axis_index("dp") * seq + pos
    tok, channels = q.shape
    groups, taps = filters.shape
    group = channels // groups
    per = LANES // group
    width = channels // CHUNKS
    subs = width // LANES
    blocks = tok // STEP
    rows = 2 * tok
    own = groups // count

    def chunk(c):
        return pl.ds(pl.multiple_of(c * width, width), width)

    def loads(c):
        return [
            pltpu.make_async_copy(src.at[:, chunk(c)], dst.at[:, chunk(c)], load.at[c, i])
            for i, (src, dst) in enumerate(((k_in, k), (v_in, v), (g_in, g), (q_in, q)))
        ]

    def stores(c):
        pairs = ((mixed, mixed_out), (grad_q, grad_q_out), (grad_k, grad_k_out), (grad_v, grad_v_out))
        return [
            pltpu.make_async_copy(src.at[:, chunk(c)], dst.at[:, chunk(c)], store.at[c, i])
            for i, (src, dst) in enumerate(pairs)
        ]

    def where(j):
        peer = lax.rem(me + j, count)
        return peer, (peer // seq, lax.rem(peer, seq))

    def to_next(c):
        return pltpu.make_async_remote_copy(
            src_ref=ext_p.at[pl.ds(tok, tok), chunk(c)], dst_ref=ext_p.at[pl.ds(0, tok), chunk(c)],
            send_sem=send_p.at[c], recv_sem=recv_p.at[c], device_id={"seq": pos + 1}, device_id_type=MESH)

    def to_previous(c):
        return pltpu.make_async_remote_copy(
            src_ref=ext_g.at[pl.ds(tok, tok), chunk(c)], dst_ref=ext_g.at[pl.ds(0, tok), chunk(c)],
            send_sem=send_g.at[c], recv_sem=recv_g.at[c], device_id={"seq": pos - 1}, device_id_type=MESH)

    def scatter(j):
        peer, place = where(j)
        return pltpu.make_async_remote_copy(
            src_ref=lag.at[peer], dst_ref=parts.at[j], send_sem=send_a.at[j],
            recv_sem=recv_a.at[j], device_id=place, device_id_type=MESH)

    def gather(j):
        return pltpu.make_async_remote_copy(
            src_ref=mine, dst_ref=gathered.at[me], send_sem=send_b.at[j],
            recv_sem=recv_b.at[j], device_id=where(j)[1], device_id_type=MESH)

    def gathered_from(j):
        return pltpu.make_async_remote_copy(
            src_ref=mine, dst_ref=gathered.at[lax.rem(me + count - j, count)], send_sem=send_b.at[j],
            recv_sem=recv_b.at[j], device_id=where(j)[1], device_id_type=MESH)

    barrier = pltpu.get_barrier_semaphore()

    @pl.loop(1, count)
    def _(j):
        pl.semaphore_signal(barrier, inc=1, device_id=where(j)[1], device_id_type=MESH)

    @pl.loop(0, CHUNKS)
    def _(c):
        for copy in loads(c):
            copy.start()

    flip = flipped(tok, BF16)
    flip2 = jnp.concatenate([flip, flip], axis=1)
    flip_taps = flipped(taps, F32)
    zeros = jnp.zeros((ext_p.shape[0] - rows, channels), BF16)
    ext_p[rows:, :] = zeros
    ext_g[rows:, :] = zeros

    @pl.when(pos == 0)
    def _():
        ext_p[0:tok, :] = jnp.zeros((tok, channels), BF16)

    @pl.when(pos == last)
    def _():
        ext_g[0:tok, :] = jnp.zeros((tok, channels), BF16)

    pl.semaphore_wait(barrier, count - 1)

    @pl.loop(0, CHUNKS)
    def _(c):
        for copy in loads(c):
            copy.wait()
        lanes = chunk(c)
        ext_p[pl.ds(tok, tok), lanes] = gated(k[:, lanes], v[:, lanes])
        ext_g[pl.ds(tok, tok), lanes] = jnp.dot(
            flip, gated(g[:, lanes], q[:, lanes]), preferred_element_type=F32).astype(BF16)

        @pl.when(pos < last)
        def _():
            to_next(c).start()

        @pl.when(pos > 0)
        def _():
            to_previous(c).start()

    @pl.loop(0, groups // per)
    def _(s):
        line = filters[pl.ds(pl.multiple_of(s * per, per), per), :].astype(F32)
        line = jnp.dot(line.astype(BF16), flip, preferred_element_type=F32)
        line = jnp.concatenate([line, jnp.zeros((per, rows - taps), F32)], axis=1)
        bands[s] = jnp.concatenate(
            [
                pltpu.roll(
                    jnp.broadcast_to(line[i : i + 1, :], (STEP, rows)), 1, axis=1, stride=1, stride_axis=0
                ).astype(BF16)
                for i in range(per)
            ],
            axis=0,
        )

    basis_rev = jnp.dot(basis[...], flip_taps, precision=HIGHEST, preferred_element_type=F32)
    owner = lax.broadcasted_iota(jnp.int32, (STEP, 2 * LANES), 1) % LANES // group

    def lag_sums(c):
        @pl.when(pos > 0)
        def _():
            to_next(c).wait_recv()

        for s in range(subs):
            lanes = pl.ds(pl.multiple_of(c * width + s * LANES, LANES), LANES)
            cross = jnp.zeros((per * STEP, rows), F32)
            for one in range(0, blocks, 2):
                two = one + 1
                at_one = tok + STEP * (blocks - 1 - one)
                at_two = tok + STEP * (blocks - 1 - two)
                cot = jnp.concatenate(
                    [ext_g[pl.ds(at_one, STEP), lanes], ext_g[pl.ds(at_two, STEP), lanes]], axis=1)
                windows = jnp.concatenate(
                    [ext_p[pl.ds(STEP * one, rows), lanes], ext_p[pl.ds(STEP * two, rows), lanes]], axis=1)
                masked = jnp.concatenate(
                    [jnp.where(owner == i, cot, jnp.zeros_like(cot)) for i in range(per)], axis=0)
                cross = cross + lax.dot_general(masked, windows, NT, preferred_element_type=F32)
            sums = []
            for i in range(per):
                skewed = pltpu.roll(
                    cross[i * STEP : (i + 1) * STEP, :], rows - STEP, axis=1, stride=1, stride_axis=0)
                sums.append(jnp.sum(skewed, axis=0, keepdims=True)[:, :tok])
            sums = jnp.concatenate(sums, axis=0).reshape(per // own, own, taps)
            lag[pl.ds((c * subs + s) * (per // own), per // own)] = sums

    def products(c):
        for s in range(subs):
            lanes = pl.ds(pl.multiple_of(c * width + s * LANES, LANES), LANES)
            band = bands[c * subs + s]
            found = []
            for a in range(blocks):
                window = jnp.concatenate(
                    [ext_p[pl.ds(STEP * a, rows), lanes], ext_g[pl.ds(STEP * a, rows), lanes]], axis=1)
                res = jnp.dot(band, window, preferred_element_type=F32)
                out = res[0:STEP, :]
                for i in range(1, per):
                    out = jnp.where(owner == i, res[i * STEP : (i + 1) * STEP, :], out)
                found.append(out)
            whole = jnp.concatenate(found, axis=0)
            conv = whole[:, :LANES]
            back = whole[:, LANES:]
            coarse = back.astype(BF16)
            fine = (back - coarse.astype(F32)).astype(BF16)
            grad_prod = jnp.dot(flip2, jnp.concatenate([coarse, fine], axis=0), preferred_element_type=F32)
            mixed[:, lanes] = (q[:, lanes].astype(F32) * conv).astype(BF16)
            grad_q[:, lanes] = (g[:, lanes].astype(F32) * conv).astype(BF16)
            grad_k[:, lanes] = (grad_prod * v[:, lanes].astype(F32)).astype(BF16)
            grad_v[:, lanes] = (grad_prod * k[:, lanes].astype(F32)).astype(BF16)
        for copy in stores(c):
            copy.start()

    @pl.loop(0, CHUNKS // 2)
    def _(h):
        for c in (2 * h, 2 * h + 1):
            lag_sums(c)

            @pl.when(pos < last)
            def _():
                to_previous(c).wait_recv()

        products(h)

    @pl.loop(1, count)
    def _(j):
        scatter(j).start()

    parts[0] = lag[me]

    @pl.loop(CHUNKS // 2, CHUNKS)
    def _(c):
        @pl.when(c == CHUNKS - CHUNKS // 4)
        def _():
            @pl.loop(1, count)
            def _(j):
                scatter(j).wait_recv()

            mine[...] = jnp.sum(parts[...], axis=0)

            @pl.loop(1, count)
            def _(j):
                gather(j).start()

        products(c)

    gathered[me] = mine[...]

    @pl.loop(1, count)
    def _(j):
        gathered_from(j).wait_recv()

    grads = gathered[...].reshape(groups, taps)
    left = lax.dot_general(basis_rev, grads, NT, precision=HIGHEST, preferred_element_type=F32)
    rank = left.shape[0]
    index = lax.broadcasted_iota(jnp.int32, left.shape, 0)
    rest = left
    ortho = jnp.zeros_like(left)
    for i in range(rank):
        column = rest[i : i + 1, :]
        norm = jnp.sum(column * column, axis=1, keepdims=True) + 1e-06
        along = jnp.sum(left * column, axis=1, keepdims=True)
        ortho = jnp.where(index == i, column / jnp.sqrt(norm), ortho)
        rest = rest - (along / norm) * column
    right = jnp.dot(ortho, grads, precision=HIGHEST, preferred_element_type=F32) * scale
    right = jnp.dot(right, flip_taps, precision=HIGHEST, preferred_element_type=F32)
    basis_next[...] = right
    low_rank[...] = lax.dot_general(ortho, right, TN, precision=HIGHEST, preferred_element_type=F32)

    @pl.loop(1, count)
    def _(j):
        scatter(j).wait_send()
        gather(j).wait_send()

    @pl.loop(0, CHUNKS)
    def _(c):
        for copy in stores(c):
            copy.wait()

        @pl.when(pos < last)
        def _():
            to_next(c).wait_send()

        @pl.when(pos > 0)
        def _():
            to_previous(c).wait_send()


def on_device(query_gate, key_gate, value_feat, filters, grad_out, basis_prev):
    q, k, v, g = query_gate[0], key_gate[0], value_feat[0], grad_out[0]
    tok, channels = q.shape
    groups, taps = filters.shape
    rank = basis_prev.shape[1]
    count = lax.axis_size("dp") * lax.axis_size("seq")
    scale = (count * tok * (channels // groups)) ** (-0.5)
    vmem = pl.BlockSpec(memory_space=pltpu.VMEM)
    anywhere = pl.BlockSpec(memory_space=pl.ANY)
    block = jax.ShapeDtypeStruct((tok, channels), BF16)
    held = pltpu.VMEM((tok, channels), BF16)
    padded = pltpu.VMEM((3 * tok - STEP, channels), BF16)
    per = LANES * groups // channels
    spread = pltpu.VMEM((count, groups // count, taps), F32)
    dma = pltpu.SemaphoreType.DMA
    mixed, grad_q, grad_k, grad_v, low_rank, basis_next = pl.pallas_call(
        functools.partial(mixer_kernel, scale),
        out_shape=(block,) * 4 + (
            jax.ShapeDtypeStruct((groups, taps), F32),
            jax.ShapeDtypeStruct((rank, taps), F32),
        ),
        in_specs=[anywhere] * 4 + [vmem] * 2,
        out_specs=[anywhere] * 4 + [vmem] * 2,
        scratch_shapes=[held] * 8 + [padded] * 2 + [
            pltpu.VMEM((groups // per, per * STEP, 2 * tok), BF16),
            spread, spread, pltpu.VMEM((groups // count, taps), F32), spread,
            dma((CHUNKS, 4)), dma((CHUNKS, 4)),
        ] + [dma((CHUNKS,))] * 4 + [dma((count,))] * 4,
        compiler_params=pltpu.CompilerParams(
            collective_id=0, has_side_effects=True, vmem_limit_bytes=56 * 2**20),
        name="mixer",
    )(q, k, v, g, filters, basis_prev.T)
    return (mixed[None], grad_q[None], grad_k[None], grad_v[None], low_rank, basis_next.T)


def solution(mesh):
    spec = P("dp", "seq", None)
    return jax.shard_map(
        on_device,
        mesh=mesh,
        in_specs=(spec, spec, spec, P(), spec, P()),
        out_specs=(spec, spec, spec, spec, P(), P()),
        check_vma=False,
    )
```

```python
import functools

import jax
import jax.numpy as jnp
from jax import lax
from jax.experimental import pallas as pl
from jax.experimental.pallas import tpu as pltpu
from jax.sharding import PartitionSpec as P

MESH = pl.DeviceIdType.MESH
HIGHEST = lax.Precision.HIGHEST
F32 = jnp.float32
BF16 = jnp.bfloat16
STEP = 32
LANES = 128
PIECES = 4
CHUNKS = 8
NT = (((1,), (1,)), ((), ()))
TN = (((0,), (0,)), ((), ()))


def flipped(size, dtype):
    rows = lax.broadcasted_iota(jnp.int32, (size, size), 0)
    cols = lax.broadcasted_iota(jnp.int32, (size, size), 1)
    return jnp.where(rows + cols == size - 1, 1.0, 0.0).astype(dtype)


def gated(left, right):
    return (left.astype(F32) * right.astype(F32)).astype(BF16)


def mixer_kernel(
    q_in, k_in, v_in, g_in, filters,
    mixed_out, grad_q_out, grad_k_out, grad_v_out, gathered,
    q, k, v, g, mixed, grad_q, grad_k, grad_v, ext_p, ext_g, bands, lag, parts, mine, shares, total,
    load, store, send_p, recv_p, send_g, recv_g, stage_send, stage_recv,
):
    dp, seq = lax.axis_size("dp"), lax.axis_size("seq")
    pos = lax.axis_index("seq")
    line_of = lax.axis_index("dp")
    last = seq - 1
    tok, channels = q.shape
    groups, taps = filters.shape
    group = channels // groups
    per = LANES // group
    width = channels // CHUNKS
    subs = width // LANES
    blocks = tok // STEP
    rows = 2 * tok
    units, unit = parts.shape[1:3]

    def chunk(c):
        return pl.ds(pl.multiple_of(c * width, width), width)

    def loads(c):
        return [
            pltpu.make_async_copy(src.at[:, chunk(c)], dst.at[:, chunk(c)], load.at[c, i])
            for i, (src, dst) in enumerate(((k_in, k), (v_in, v), (g_in, g), (q_in, q)))
        ]

    def stores(c):
        pairs = ((mixed, mixed_out), (grad_q, grad_q_out), (grad_k, grad_k_out), (grad_v, grad_v_out))
        return [
            pltpu.make_async_copy(src.at[:, chunk(c)], dst.at[:, chunk(c)], store.at[c, i])
            for i, (src, dst) in enumerate(pairs)
        ]

    def along_seq(j):
        return lax.rem(pos + j, seq)

    def along_dp(j):
        return lax.rem(line_of + j, dp)

    def to_next(c):
        return pltpu.make_async_remote_copy(
            src_ref=ext_p.at[pl.ds(tok, tok), chunk(c)], dst_ref=ext_p.at[pl.ds(0, tok), chunk(c)],
            send_sem=send_p.at[c], recv_sem=recv_p.at[c], device_id={"seq": pos + 1}, device_id_type=MESH)

    def to_previous(c):
        return pltpu.make_async_remote_copy(
            src_ref=ext_g.at[pl.ds(tok, tok), chunk(c)], dst_ref=ext_g.at[pl.ds(0, tok), chunk(c)],
            send_sem=send_g.at[c], recv_sem=recv_g.at[c], device_id={"seq": pos - 1}, device_id_type=MESH)

    def scatter(j):
        peer = along_seq(j)
        return pltpu.make_async_remote_copy(
            src_ref=lag.at[pl.ds(peer * units, units)], dst_ref=parts.at[j], send_sem=stage_send.at[0],
            recv_sem=stage_recv.at[0], device_id={"seq": peer}, device_id_type=MESH)

    def exchange(j):
        return pltpu.make_async_remote_copy(
            src_ref=mine, dst_ref=shares.at[line_of], send_sem=stage_send.at[1],
            recv_sem=stage_recv.at[1], device_id={"dp": along_dp(j)}, device_id_type=MESH)

    def gather(j):
        return pltpu.make_async_remote_copy(
            src_ref=total, dst_ref=gathered.at[pos], send_sem=stage_send.at[2],
            recv_sem=stage_recv.at[2], device_id={"seq": along_seq(j)}, device_id_type=MESH)

    def all_of(sems, stage):
        size = shares if stage == 1 else parts
        span = size.at[pl.ds(1, size.shape[0] - 1)]
        pltpu.make_async_copy(span, span, sems.at[stage]).wait()

    barrier = pltpu.get_barrier_semaphore()

    @pl.loop(0, CHUNKS)
    def _(c):
        for copy in loads(c):
            copy.start()

    @pl.loop(1, seq)
    def _(j):
        pl.semaphore_signal(barrier, inc=1, device_id={"seq": along_seq(j)}, device_id_type=MESH)

    @pl.loop(1, dp)
    def _(j):
        pl.semaphore_signal(barrier, inc=1, device_id={"dp": along_dp(j)}, device_id_type=MESH)

    flip = flipped(tok, BF16)
    flip2 = jnp.concatenate([flip, flip], axis=1)
    zeros = jnp.zeros((ext_p.shape[0] - rows, channels), BF16)
    ext_p[rows:, :] = zeros
    ext_g[rows:, :] = zeros

    @pl.when(pos == 0)
    def _():
        ext_p[0:tok, :] = jnp.zeros((tok, channels), BF16)

    @pl.when(pos == last)
    def _():
        ext_g[0:tok, :] = jnp.zeros((tok, channels), BF16)

    pl.semaphore_wait(barrier, seq + dp - 2)

    @pl.loop(0, CHUNKS)
    def _(c):
        for copy in loads(c):
            copy.wait()
        lanes = chunk(c)
        ext_p[pl.ds(tok, tok), lanes] = gated(k[:, lanes], v[:, lanes])
        ext_g[pl.ds(tok, tok), lanes] = jnp.dot(
            flip, gated(g[:, lanes], q[:, lanes]), preferred_element_type=F32).astype(BF16)

        @pl.when(pos < last)
        def _():
            to_next(c).start()

        @pl.when(pos > 0)
        def _():
            to_previous(c).start()

    @pl.loop(0, groups // per)
    def _(s):
        line = filters[pl.ds(pl.multiple_of(s * per, per), per), :].astype(F32)
        line = jnp.dot(line.astype(BF16), flip, preferred_element_type=F32)
        line = jnp.concatenate([line, jnp.zeros((per, rows - taps), F32)], axis=1)
        bands[s] = jnp.concatenate(
            [
                pltpu.roll(
                    jnp.broadcast_to(line[i : i + 1, :], (STEP, rows)), 1, axis=1, stride=1, stride_axis=0
                ).astype(BF16)
                for i in range(per)
            ],
            axis=0,
        )

    owner = lax.broadcasted_iota(jnp.int32, (STEP, 2 * LANES), 1) % LANES // group

    def lag_sums(c):
        @pl.when(pos > 0)
        def _():
            to_next(c).wait_recv()

        for s in range(subs):
            lanes = pl.ds(pl.multiple_of(c * width + s * LANES, LANES), LANES)
            cross = jnp.zeros((per * STEP, rows), F32)
            for one in range(0, blocks, 2):
                two = one + 1
                at_one = tok + STEP * (blocks - 1 - one)
                at_two = tok + STEP * (blocks - 1 - two)
                cot = jnp.concatenate(
                    [ext_g[pl.ds(at_one, STEP), lanes], ext_g[pl.ds(at_two, STEP), lanes]], axis=1)
                windows = jnp.concatenate(
                    [ext_p[pl.ds(STEP * one, rows), lanes], ext_p[pl.ds(STEP * two, rows), lanes]], axis=1)
                masked = jnp.concatenate(
                    [jnp.where(owner == i, cot, jnp.zeros_like(cot)) for i in range(per)], axis=0)
                cross = cross + lax.dot_general(masked, windows, NT, preferred_element_type=F32)
            sums = []
            for i in range(per):
                skewed = pltpu.roll(
                    cross[i * STEP : (i + 1) * STEP, :], rows - STEP, axis=1, stride=1, stride_axis=0)
                sums.append(jnp.sum(skewed, axis=0, keepdims=True)[:, :tok])
            sums = jnp.concatenate(sums, axis=0).reshape(per // unit, unit, taps)
            lag[pl.ds((c * subs + s) * (per // unit), per // unit)] = sums

    def products(c):
        for s in range(subs):
            lanes = pl.ds(pl.multiple_of(c * width + s * LANES, LANES), LANES)
            band = bands[c * subs + s]
            found = []
            for a in range(blocks):
                window = jnp.concatenate(
                    [ext_p[pl.ds(STEP * a, rows), lanes], ext_g[pl.ds(STEP * a, rows), lanes]], axis=1)
                res = jnp.dot(band, window, preferred_element_type=F32)
                out = res[0:STEP, :]
                for i in range(1, per):
                    out = jnp.where(owner == i, res[i * STEP : (i + 1) * STEP, :], out)
                found.append(out)
            whole = jnp.concatenate(found, axis=0)
            conv = whole[:, :LANES]
            back = whole[:, LANES:]
            coarse = back.astype(BF16)
            fine = (back - coarse.astype(F32)).astype(BF16)
            grad_prod = jnp.dot(flip2, jnp.concatenate([coarse, fine], axis=0), preferred_element_type=F32)
            mixed[:, lanes] = (q[:, lanes].astype(F32) * conv).astype(BF16)
            grad_q[:, lanes] = (g[:, lanes].astype(F32) * conv).astype(BF16)
            grad_k[:, lanes] = (grad_prod * v[:, lanes].astype(F32)).astype(BF16)
            grad_v[:, lanes] = (grad_prod * k[:, lanes].astype(F32)).astype(BF16)
        for copy in stores(c):
            copy.start()

    @pl.loop(0, CHUNKS // 2)
    def _(h):
        for c in (2 * h, 2 * h + 1):
            lag_sums(c)

            @pl.when(pos < last)
            def _():
                to_previous(c).wait_recv()

        products(h)

    @pl.loop(1, seq)
    def _(j):
        scatter(j).start()

    parts[0] = lag[pl.ds(pos * units, units)]

    @pl.loop(CHUNKS // 2, CHUNKS)
    def _(c):
        @pl.when(c == CHUNKS - 2)
        def _():
            all_of(stage_recv, 0)
            mine[...] = jnp.sum(parts[...], axis=0)

            @pl.loop(1, dp)
            def _(j):
                exchange(j).start()

            shares[line_of] = mine[...]

        @pl.when(c == CHUNKS - 1)
        def _():
            all_of(stage_recv, 1)
            total[...] = jnp.sum(shares[...], axis=0)

            @pl.loop(1, seq)
            def _(j):
                gather(j).start()

            gathered[pos] = total[...]

        products(c)

    all_of(stage_recv, 2)
    for stage in range(3):
        all_of(stage_send, stage)

    @pl.loop(0, CHUNKS)
    def _(c):
        for copy in stores(c):
            copy.wait()

        @pl.when(pos < last)
        def _():
            to_next(c).wait_send()

        @pl.when(pos > 0)
        def _():
            to_previous(c).wait_send()


def factor_kernel(scale, grads, basis, *refs):
    moved = tuple(zip(refs[:4], refs[4:8]))
    low_rank, basis_next, sems = refs[8:]
    tok = refs[0].shape[0]
    piece = tok // PIECES

    def moves():
        return [
            pltpu.make_async_copy(
                src.at[pl.ds(p * piece, piece)], dst.at[pl.ds(p * piece, piece)], sems.at[i, p])
            for i, (src, dst) in enumerate(moved)
            for p in range(PIECES)
        ]

    for copy in moves():
        copy.start()
    taps = grads.shape[1]
    flip_taps = flipped(taps, F32)
    basis_rev = jnp.dot(basis[...], flip_taps, precision=HIGHEST, preferred_element_type=F32)
    left = lax.dot_general(basis_rev, grads[...], NT, precision=HIGHEST, preferred_element_type=F32)
    rank = left.shape[0]
    index = lax.broadcasted_iota(jnp.int32, left.shape, 0)
    rest = left
    ortho = jnp.zeros_like(left)
    for i in range(rank):
        column = rest[i : i + 1, :]
        norm = jnp.sum(column * column, axis=1, keepdims=True) + 1e-06
        along = jnp.sum(left * column, axis=1, keepdims=True)
        ortho = jnp.where(index == i, column / jnp.sqrt(norm), ortho)
        rest = rest - (along / norm) * column
    right = jnp.dot(ortho, grads[...], precision=HIGHEST, preferred_element_type=F32) * scale
    right = jnp.dot(right, flip_taps, precision=HIGHEST, preferred_element_type=F32)
    basis_next[...] = right
    low_rank[...] = lax.dot_general(ortho, right, TN, precision=HIGHEST, preferred_element_type=F32)
    for copy in moves():
        copy.wait()


def on_device(query_gate, key_gate, value_feat, filters, grad_out, basis_prev):
    q, k, v, g = query_gate[0], key_gate[0], value_feat[0], grad_out[0]
    tok, channels = q.shape
    groups, taps = filters.shape
    rank = basis_prev.shape[1]
    scale = (lax.axis_size("dp") * lax.axis_size("seq") * tok * (channels // groups)) ** (-0.5)
    vmem = pl.BlockSpec(memory_space=pltpu.VMEM)
    anywhere = pl.BlockSpec(memory_space=pl.ANY)
    block = jax.ShapeDtypeStruct((tok, channels), BF16)
    held = pltpu.VMEM((tok, channels), BF16)
    padded = pltpu.VMEM((3 * tok - STEP, channels), BF16)
    per = LANES * groups // channels
    dp, seq = lax.axis_size("dp"), lax.axis_size("seq")
    unit = min(per, groups // seq)
    share = (groups // seq // unit, unit, taps)
    dma = pltpu.SemaphoreType.DMA
    *results, grads = pl.pallas_call(
        mixer_kernel,
        out_shape=(block,) * 4 + (jax.ShapeDtypeStruct((seq,) + share, F32),),
        in_specs=[anywhere] * 4 + [vmem],
        out_specs=[anywhere] * 4 + [vmem],
        scratch_shapes=[held] * 8 + [padded] * 2 + [
            pltpu.VMEM((groups // per, per * STEP, 2 * tok), BF16),
            pltpu.VMEM((groups // unit, unit, taps), F32),
            pltpu.VMEM((seq,) + share, F32), pltpu.VMEM(share, F32),
            pltpu.VMEM((dp,) + share, F32), pltpu.VMEM(share, F32),
            dma((CHUNKS, 4)), dma((CHUNKS, 4)),
        ] + [dma((CHUNKS,))] * 4 + [dma((3,))] * 2,
        compiler_params=pltpu.CompilerParams(
            collective_id=0, has_side_effects=True, vmem_limit_bytes=56 * 2**20),
        name="mixer",
    )(q, k, v, g, filters)
    mixed, grad_q, grad_k, grad_v, low_rank, basis_next = pl.pallas_call(
        functools.partial(factor_kernel, scale),
        out_shape=(block,) * 4 + (
            jax.ShapeDtypeStruct((groups, taps), F32),
            jax.ShapeDtypeStruct((rank, taps), F32),
        ),
        in_specs=[vmem] * 2 + [anywhere] * 4,
        out_specs=[anywhere] * 4 + [vmem] * 2,
        scratch_shapes=[dma((4, PIECES))],
        compiler_params=pltpu.CompilerParams(vmem_limit_bytes=56 * 2**20),
        name="factors",
    )(grads.reshape(groups, taps), basis_prev.T, *results)
    return (mixed[None], grad_q[None], grad_k[None], grad_v[None], low_rank, basis_next.T)


def solution(mesh):
    spec = P("dp", "seq", None)
    return jax.shard_map(
        on_device,
        mesh=mesh,
        in_specs=(spec, spec, spec, P(), spec, P()),
        out_specs=(spec, spec, spec, spec, P(), P()),
        check_vma=False,
    )
```

```python
import functools

import jax
import jax.numpy as jnp
from jax import lax
from jax.experimental import pallas as pl
from jax.experimental.pallas import tpu as pltpu
from jax.sharding import PartitionSpec as P

MESH = pl.DeviceIdType.MESH
HIGHEST = lax.Precision.HIGHEST
F32 = jnp.float32
BF16 = jnp.bfloat16
STEP = 32
LANES = 128
PIECES = 4
FLIGHT = 3
CHUNKS = 8
NT = (((1,), (1,)), ((), ()))
TN = (((0,), (0,)), ((), ()))


def flipped(size, dtype):
    rows = lax.broadcasted_iota(jnp.int32, (size, size), 0)
    cols = lax.broadcasted_iota(jnp.int32, (size, size), 1)
    return jnp.where(rows + cols == size - 1, 1.0, 0.0).astype(dtype)


def gated(left, right):
    return (left.astype(F32) * right.astype(F32)).astype(BF16)


def mixer_kernel(
    q_in, k_in, v_in, g_in, filters,
    mixed_out, grad_q_out, grad_k_out, grad_v_out, gathered,
    q, k, v, g, mixed, grad_q, grad_k, grad_v, ext_p, ext_g, bands, lag, parts, mine, shares, total,
    load, store, send_p, recv_p, send_g, recv_g, stage_send, stage_recv,
):
    dp, seq = lax.axis_size("dp"), lax.axis_size("seq")
    pos = lax.axis_index("seq")
    line_of = lax.axis_index("dp")
    last = seq - 1
    tok, channels = q.shape
    groups, taps = filters.shape
    group = channels // groups
    per = LANES // group
    width = channels // CHUNKS
    subs = width // LANES
    blocks = tok // STEP
    rows = 2 * tok
    units, unit = parts.shape[1:3]

    def chunk(c):
        return pl.ds(pl.multiple_of(c * width, width), width)

    def loads(c):
        return [
            pltpu.make_async_copy(src.at[:, chunk(c)], dst.at[:, chunk(c)], load.at[c, i])
            for i, (src, dst) in enumerate(((k_in, k), (v_in, v), (g_in, g), (q_in, q)))
        ]

    def stores(c):
        pairs = ((mixed, mixed_out), (grad_q, grad_q_out), (grad_k, grad_k_out), (grad_v, grad_v_out))
        return [
            pltpu.make_async_copy(src.at[:, chunk(c)], dst.at[:, chunk(c)], store.at[c, i])
            for i, (src, dst) in enumerate(pairs)
        ]

    def along_seq(j):
        return lax.rem(pos + j, seq)

    def along_dp(j):
        return lax.rem(line_of + j, dp)

    def to_next(c):
        return pltpu.make_async_remote_copy(
            src_ref=ext_p.at[pl.ds(tok, tok), chunk(c)], dst_ref=ext_p.at[pl.ds(0, tok), chunk(c)],
            send_sem=send_p.at[c], recv_sem=recv_p.at[c], device_id={"seq": pos + 1}, device_id_type=MESH)

    def to_previous(c):
        return pltpu.make_async_remote_copy(
            src_ref=ext_g.at[pl.ds(tok, tok), chunk(c)], dst_ref=ext_g.at[pl.ds(0, tok), chunk(c)],
            send_sem=send_g.at[c], recv_sem=recv_g.at[c], device_id={"seq": pos - 1}, device_id_type=MESH)

    def scatter(j):
        peer = along_seq(j)
        return pltpu.make_async_remote_copy(
            src_ref=lag.at[pl.ds(peer * units, units)], dst_ref=parts.at[j], send_sem=stage_send.at[0],
            recv_sem=stage_recv.at[0], device_id={"seq": peer}, device_id_type=MESH)

    def exchange(j):
        return pltpu.make_async_remote_copy(
            src_ref=mine, dst_ref=shares.at[line_of], send_sem=stage_send.at[1],
            recv_sem=stage_recv.at[1], device_id={"dp": along_dp(j)}, device_id_type=MESH)

    def gather(j):
        return pltpu.make_async_remote_copy(
            src_ref=total, dst_ref=gathered.at[pos], send_sem=stage_send.at[2],
            recv_sem=stage_recv.at[2], device_id={"seq": along_seq(j)}, device_id_type=MESH)

    def all_of(sems, stage):
        size = shares if stage == 1 else parts
        span = size.at[pl.ds(1, size.shape[0] - 1)]
        pltpu.make_async_copy(span, span, sems.at[stage]).wait()

    barrier = pltpu.get_barrier_semaphore()

    @pl.loop(0, CHUNKS)
    def _(c):
        for copy in loads(c):
            copy.start()

    @pl.loop(1, seq)
    def _(j):
        pl.semaphore_signal(barrier, inc=1, device_id={"seq": along_seq(j)}, device_id_type=MESH)

    @pl.loop(1, dp)
    def _(j):
        pl.semaphore_signal(barrier, inc=1, device_id={"dp": along_dp(j)}, device_id_type=MESH)

    flip = flipped(tok, BF16)
    flip2 = jnp.concatenate([flip, flip], axis=1)
    zeros = jnp.zeros((ext_p.shape[0] - rows, channels), BF16)
    ext_p[rows:, :] = zeros
    ext_g[rows:, :] = zeros

    @pl.when(pos == 0)
    def _():
        ext_p[0:tok, :] = jnp.zeros((tok, channels), BF16)

    @pl.when(pos == last)
    def _():
        ext_g[0:tok, :] = jnp.zeros((tok, channels), BF16)

    def gates(c):
        for copy in loads(c):
            copy.wait()
        lanes = chunk(c)
        ext_p[pl.ds(tok, tok), lanes] = gated(k[:, lanes], v[:, lanes])
        ext_g[pl.ds(tok, tok), lanes] = jnp.dot(
            flip, gated(g[:, lanes], q[:, lanes]), preferred_element_type=F32).astype(BF16)

    def send(c):
        @pl.when(pos < last)
        def _():
            to_next(c).start()

        @pl.when(pos > 0)
        def _():
            to_previous(c).start()

    def sent(c):
        @pl.when(pos < last)
        def _():
            to_next(c).wait_send()

        @pl.when(pos > 0)
        def _():
            to_previous(c).wait_send()

    gates(0)
    pl.semaphore_wait(barrier, seq + dp - 2)
    send(0)

    @pl.loop(1, CHUNKS)
    def _(c):
        gates(c)

        @pl.when(c < FLIGHT)
        def _():
            send(c)

    @pl.loop(0, groups // per)
    def _(s):
        line = filters[pl.ds(pl.multiple_of(s * per, per), per), :].astype(F32)
        line = jnp.dot(line.astype(BF16), flip, preferred_element_type=F32)
        line = jnp.concatenate([line, jnp.zeros((per, rows - taps), F32)], axis=1)
        bands[s] = jnp.concatenate(
            [
                pltpu.roll(
                    jnp.broadcast_to(line[i : i + 1, :], (STEP, rows)), 1, axis=1, stride=1, stride_axis=0
                ).astype(BF16)
                for i in range(per)
            ],
            axis=0,
        )

    owner = lax.broadcasted_iota(jnp.int32, (STEP, 2 * LANES), 1) % LANES // group

    def lag_sums(c):
        @pl.when(pos > 0)
        def _():
            to_next(c).wait_recv()

        for s in range(subs):
            lanes = pl.ds(pl.multiple_of(c * width + s * LANES, LANES), LANES)
            cross = jnp.zeros((per * STEP, rows), F32)
            for one in range(0, blocks, 2):
                two = one + 1
                at_one = tok + STEP * (blocks - 1 - one)
                at_two = tok + STEP * (blocks - 1 - two)
                cot = jnp.concatenate(
                    [ext_g[pl.ds(at_one, STEP), lanes], ext_g[pl.ds(at_two, STEP), lanes]], axis=1)
                windows = jnp.concatenate(
                    [ext_p[pl.ds(STEP * one, rows), lanes], ext_p[pl.ds(STEP * two, rows), lanes]], axis=1)
                masked = jnp.concatenate(
                    [jnp.where(owner == i, cot, jnp.zeros_like(cot)) for i in range(per)], axis=0)
                cross = cross + lax.dot_general(masked, windows, NT, preferred_element_type=F32)
            sums = []
            for i in range(per):
                skewed = pltpu.roll(
                    cross[i * STEP : (i + 1) * STEP, :], rows - STEP, axis=1, stride=1, stride_axis=0)
                sums.append(jnp.sum(skewed, axis=0, keepdims=True)[:, :tok])
            sums = jnp.concatenate(sums, axis=0).reshape(per // unit, unit, taps)
            lag[pl.ds((c * subs + s) * (per // unit), per // unit)] = sums

    def products(c):
        for s in range(subs):
            lanes = pl.ds(pl.multiple_of(c * width + s * LANES, LANES), LANES)
            band = bands[c * subs + s]
            found = []
            for a in range(blocks):
                window = jnp.concatenate(
                    [ext_p[pl.ds(STEP * a, rows), lanes], ext_g[pl.ds(STEP * a, rows), lanes]], axis=1)
                res = jnp.dot(band, window, preferred_element_type=F32)
                out = res[0:STEP, :]
                for i in range(1, per):
                    out = jnp.where(owner == i, res[i * STEP : (i + 1) * STEP, :], out)
                found.append(out)
            whole = jnp.concatenate(found, axis=0)
            conv = whole[:, :LANES]
            back = whole[:, LANES:]
            coarse = back.astype(BF16)
            fine = (back - coarse.astype(F32)).astype(BF16)
            grad_prod = jnp.dot(flip2, jnp.concatenate([coarse, fine], axis=0), preferred_element_type=F32)
            mixed[:, lanes] = (q[:, lanes].astype(F32) * conv).astype(BF16)
            grad_q[:, lanes] = (g[:, lanes].astype(F32) * conv).astype(BF16)
            grad_k[:, lanes] = (grad_prod * v[:, lanes].astype(F32)).astype(BF16)
            grad_v[:, lanes] = (grad_prod * k[:, lanes].astype(F32)).astype(BF16)
        for copy in stores(c):
            copy.start()

    @pl.loop(0, CHUNKS // 2)
    def _(h):
        for c in (2 * h, 2 * h + 1):
            sent(c)

            @pl.when(c + FLIGHT < CHUNKS)
            def _():
                send(c + FLIGHT)

            lag_sums(c)

            @pl.when(pos < last)
            def _():
                to_previous(c).wait_recv()

        products(h)

    @pl.loop(1, seq)
    def _(j):
        scatter(j).start()

    parts[0] = lag[pl.ds(pos * units, units)]

    @pl.loop(CHUNKS // 2, CHUNKS)
    def _(c):
        @pl.when(c == CHUNKS - 2)
        def _():
            all_of(stage_recv, 0)
            mine[...] = jnp.sum(parts[...], axis=0)

            @pl.loop(1, dp)
            def _(j):
                exchange(j).start()

            shares[line_of] = mine[...]

        @pl.when(c == CHUNKS - 1)
        def _():
            all_of(stage_recv, 1)
            total[...] = jnp.sum(shares[...], axis=0)

            @pl.loop(1, seq)
            def _(j):
                gather(j).start()

            gathered[pos] = total[...]

        products(c)

    all_of(stage_recv, 2)
    for stage in range(3):
        all_of(stage_send, stage)

    @pl.loop(0, CHUNKS)
    def _(c):
        for copy in stores(c):
            copy.wait()


def factor_kernel(scale, grads, basis, *refs):
    moved = tuple(zip(refs[:4], refs[4:8]))
    low_rank, basis_next = refs[8:10]
    held, sem_in, sem_out = refs[10:]
    piece = refs[0].shape[0] // PIECES

    def moves(inward):
        copies = []
        for i, (src, dst) in enumerate(moved):
            for p in range(PIECES):
                part = pl.ds(p * piece, piece)
                ends = (src.at[part], held.at[i, part]) if inward else (held.at[i, part], dst.at[part])
                copies.append(pltpu.make_async_copy(*ends, (sem_in if inward else sem_out).at[i, p]))
        return copies

    for copy in moves(True):
        copy.start()
    taps = grads.shape[1]
    flip_taps = flipped(taps, F32)
    basis_rev = jnp.dot(basis[...], flip_taps, precision=HIGHEST, preferred_element_type=F32)
    left = lax.dot_general(basis_rev, grads[...], NT, precision=HIGHEST, preferred_element_type=F32)
    rank = left.shape[0]
    index = lax.broadcasted_iota(jnp.int32, left.shape, 0)
    rest = left
    ortho = jnp.zeros_like(left)
    for i in range(rank):
        if i == 2:
            for arrived, leaving in zip(moves(True), moves(False)):
                arrived.wait()
                leaving.start()
        column = rest[i : i + 1, :]
        norm = jnp.sum(column * column, axis=1, keepdims=True) + 1e-06
        along = jnp.sum(left * column, axis=1, keepdims=True)
        ortho = jnp.where(index == i, column / jnp.sqrt(norm), ortho)
        rest = rest - (along / norm) * column
    right = jnp.dot(ortho, grads[...], precision=HIGHEST, preferred_element_type=F32) * scale
    right = jnp.dot(right, flip_taps, precision=HIGHEST, preferred_element_type=F32)
    basis_next[...] = right
    low_rank[...] = lax.dot_general(ortho, right, TN, precision=HIGHEST, preferred_element_type=F32)
    for copy in moves(False):
        copy.wait()


def on_device(query_gate, key_gate, value_feat, filters, grad_out, basis_prev):
    q, k, v, g = query_gate[0], key_gate[0], value_feat[0], grad_out[0]
    tok, channels = q.shape
    groups, taps = filters.shape
    rank = basis_prev.shape[1]
    scale = (lax.axis_size("dp") * lax.axis_size("seq") * tok * (channels // groups)) ** (-0.5)
    vmem = pl.BlockSpec(memory_space=pltpu.VMEM)
    anywhere = pl.BlockSpec(memory_space=pl.ANY)
    block = jax.ShapeDtypeStruct((tok, channels), BF16)
    held = pltpu.VMEM((tok, channels), BF16)
    padded = pltpu.VMEM((3 * tok - STEP, channels), BF16)
    per = LANES * groups // channels
    dp, seq = lax.axis_size("dp"), lax.axis_size("seq")
    unit = min(per, groups // seq)
    share = (groups // seq // unit, unit, taps)
    dma = pltpu.SemaphoreType.DMA
    *results, grads = pl.pallas_call(
        mixer_kernel,
        out_shape=(block,) * 4 + (jax.ShapeDtypeStruct((seq,) + share, F32),),
        in_specs=[anywhere] * 4 + [vmem],
        out_specs=[anywhere] * 4 + [vmem],
        scratch_shapes=[held] * 8 + [padded] * 2 + [
            pltpu.VMEM((groups // per, per * STEP, 2 * tok), BF16),
            pltpu.VMEM((groups // unit, unit, taps), F32),
            pltpu.VMEM((seq,) + share, F32), pltpu.VMEM(share, F32),
            pltpu.VMEM((dp,) + share, F32), pltpu.VMEM(share, F32),
            dma((CHUNKS, 4)), dma((CHUNKS, 4)),
        ] + [dma((CHUNKS,))] * 4 + [dma((3,))] * 2,
        compiler_params=pltpu.CompilerParams(
            collective_id=0, has_side_effects=True, vmem_limit_bytes=56 * 2**20),
        name="mixer",
    )(q, k, v, g, filters)
    mixed, grad_q, grad_k, grad_v, low_rank, basis_next = pl.pallas_call(
        functools.partial(factor_kernel, scale),
        out_shape=(block,) * 4 + (
            jax.ShapeDtypeStruct((groups, taps), F32),
            jax.ShapeDtypeStruct((rank, taps), F32),
        ),
        in_specs=[vmem] * 2 + [anywhere] * 4,
        out_specs=[anywhere] * 4 + [vmem] * 2,
        scratch_shapes=[pltpu.VMEM((4, tok, channels), BF16), dma((4, PIECES)), dma((4, PIECES))],
        compiler_params=pltpu.CompilerParams(vmem_limit_bytes=56 * 2**20),
        name="factors",
    )(grads.reshape(groups, taps), basis_prev.T, *results)
    return (mixed[None], grad_q[None], grad_k[None], grad_v[None], low_rank, basis_next.T)


def solution(mesh):
    spec = P("dp", "seq", None)
    return jax.shard_map(
        on_device,
        mesh=mesh,
        in_specs=(spec, spec, spec, P(), spec, P()),
        out_specs=(spec, spec, spec, spec, P(), P()),
        check_vma=False,
    )
```

```python
import functools

import jax
import jax.numpy as jnp
from jax import lax
from jax.experimental import pallas as pl
from jax.experimental.pallas import tpu as pltpu
from jax.sharding import PartitionSpec as P

MESH = pl.DeviceIdType.MESH
HIGHEST = lax.Precision.HIGHEST
F32 = jnp.float32
BF16 = jnp.bfloat16
STEP = 32
LANES = 128
PIECES = 4
FLIGHT = 3
CHUNKS = 8
NT = (((1,), (1,)), ((), ()))
TN = (((0,), (0,)), ((), ()))


def flipped(size, dtype):
    rows = lax.broadcasted_iota(jnp.int32, (size, size), 0)
    cols = lax.broadcasted_iota(jnp.int32, (size, size), 1)
    return jnp.where(rows + cols == size - 1, 1.0, 0.0).astype(dtype)


def gated(left, right):
    return (left.astype(F32) * right.astype(F32)).astype(BF16)


def mixer_kernel(
    q_in, k_in, v_in, g_in, filters,
    mixed_out, grad_q_out, grad_k_out, grad_v_out, gathered,
    q, k, v, g, mixed, grad_q, grad_k, grad_v, ext_p, ext_g, lines, lag, parts, mine, shares, total,
    load, store, send_p, recv_p, send_g, recv_g, stage_send, stage_recv,
):
    dp, seq = lax.axis_size("dp"), lax.axis_size("seq")
    pos = lax.axis_index("seq")
    line_of = lax.axis_index("dp")
    last = seq - 1
    tok, channels = q.shape
    groups, taps = filters.shape
    group = channels // groups
    per = LANES // group
    width = channels // CHUNKS
    subs = width // LANES
    blocks = tok // STEP
    rows = 2 * tok
    units, unit = parts.shape[1:3]

    def chunk(c):
        return pl.ds(pl.multiple_of(c * width, width), width)

    def loads(c):
        return [
            pltpu.make_async_copy(src.at[:, chunk(c)], dst.at[:, chunk(c)], load.at[c, i])
            for i, (src, dst) in enumerate(((k_in, k), (v_in, v), (g_in, g), (q_in, q)))
        ]

    def stores(c):
        pairs = ((mixed, mixed_out), (grad_q, grad_q_out), (grad_k, grad_k_out), (grad_v, grad_v_out))
        return [
            pltpu.make_async_copy(src.at[:, chunk(c)], dst.at[:, chunk(c)], store.at[c, i])
            for i, (src, dst) in enumerate(pairs)
        ]

    def along_seq(j):
        return lax.rem(pos + j, seq)

    def along_dp(j):
        return lax.rem(line_of + j, dp)

    def to_next(c):
        return pltpu.make_async_remote_copy(
            src_ref=ext_p.at[pl.ds(tok, tok), chunk(c)], dst_ref=ext_p.at[pl.ds(0, tok), chunk(c)],
            send_sem=send_p.at[c], recv_sem=recv_p.at[c], device_id={"seq": pos + 1}, device_id_type=MESH)

    def to_previous(c):
        return pltpu.make_async_remote_copy(
            src_ref=ext_g.at[pl.ds(tok, tok), chunk(c)], dst_ref=ext_g.at[pl.ds(0, tok), chunk(c)],
            send_sem=send_g.at[c], recv_sem=recv_g.at[c], device_id={"seq": pos - 1}, device_id_type=MESH)

    def scatter(j):
        peer = along_seq(j)
        return pltpu.make_async_remote_copy(
            src_ref=lag.at[pl.ds(peer * units, units)], dst_ref=parts.at[j], send_sem=stage_send.at[0],
            recv_sem=stage_recv.at[0], device_id={"seq": peer}, device_id_type=MESH)

    def exchange(j):
        return pltpu.make_async_remote_copy(
            src_ref=mine, dst_ref=shares.at[line_of], send_sem=stage_send.at[1],
            recv_sem=stage_recv.at[1], device_id={"dp": along_dp(j)}, device_id_type=MESH)

    def gather(j):
        return pltpu.make_async_remote_copy(
            src_ref=total, dst_ref=gathered.at[pos], send_sem=stage_send.at[2],
            recv_sem=stage_recv.at[2], device_id={"seq": along_seq(j)}, device_id_type=MESH)

    def all_of(sems, stage):
        size = shares if stage == 1 else parts
        span = size.at[pl.ds(1, size.shape[0] - 1)]
        pltpu.make_async_copy(span, span, sems.at[stage]).wait()

    barrier = pltpu.get_barrier_semaphore()

    @pl.loop(0, CHUNKS)
    def _(c):
        for copy in loads(c):
            copy.start()

    @pl.loop(1, seq)
    def _(j):
        pl.semaphore_signal(barrier, inc=1, device_id={"seq": along_seq(j)}, device_id_type=MESH)

    @pl.loop(1, dp)
    def _(j):
        pl.semaphore_signal(barrier, inc=1, device_id={"dp": along_dp(j)}, device_id_type=MESH)

    flip = flipped(tok, BF16)
    flip2 = jnp.concatenate([flip, flip], axis=1)
    lines[:, :taps] = jnp.dot(filters[...], flip, preferred_element_type=F32)
    lines[:, taps:] = jnp.zeros((groups, rows - taps), F32)
    zeros = jnp.zeros((ext_p.shape[0] - rows, channels), BF16)
    ext_p[rows:, :] = zeros
    ext_g[rows:, :] = zeros

    @pl.when(pos == 0)
    def _():
        ext_p[0:tok, :] = jnp.zeros((tok, channels), BF16)

    @pl.when(pos == last)
    def _():
        ext_g[0:tok, :] = jnp.zeros((tok, channels), BF16)

    def gates(c):
        lanes = chunk(c)
        ext_p[pl.ds(tok, tok), lanes] = gated(k[:, lanes], v[:, lanes])
        ext_g[pl.ds(tok, tok), lanes] = jnp.dot(
            flip, gated(g[:, lanes], q[:, lanes]), preferred_element_type=F32).astype(BF16)

    def send(c):
        @pl.when(pos < last)
        def _():
            to_next(c).start()

        @pl.when(pos > 0)
        def _():
            to_previous(c).start()

    def sent(c):
        @pl.when(pos < last)
        def _():
            to_next(c).wait_send()

        @pl.when(pos > 0)
        def _():
            to_previous(c).wait_send()

    for low, high in ((0, 1), (1, FLIGHT), (FLIGHT, CHUNKS)):
        for c in range(low, high):
            for copy in loads(c):
                copy.wait()
        for c in range(low, high):
            gates(c)
        if low == 0:
            pl.semaphore_wait(barrier, seq + dp - 2)
        if low < FLIGHT:
            for c in range(low, high):
                send(c)

    owner = lax.broadcasted_iota(jnp.int32, (STEP, 2 * LANES), 1) % LANES // group

    def lag_sums(c):
        for s in range(subs):
            lanes = pl.ds(pl.multiple_of(c * width + s * LANES, LANES), LANES)
            cross = jnp.zeros((per * STEP, rows), F32)
            for one in range(0, blocks, 2):
                two = one + 1
                at_one = tok + STEP * (blocks - 1 - one)
                at_two = tok + STEP * (blocks - 1 - two)
                cot = jnp.concatenate(
                    [ext_g[pl.ds(at_one, STEP), lanes], ext_g[pl.ds(at_two, STEP), lanes]], axis=1)
                windows = jnp.concatenate(
                    [ext_p[pl.ds(STEP * one, rows), lanes], ext_p[pl.ds(STEP * two, rows), lanes]], axis=1)
                masked = jnp.concatenate(
                    [jnp.where(owner == i, cot, jnp.zeros_like(cot)) for i in range(per)], axis=0)
                cross = cross + lax.dot_general(masked, windows, NT, preferred_element_type=F32)
            sums = []
            for i in range(per):
                skewed = pltpu.roll(
                    cross[i * STEP : (i + 1) * STEP, :], rows - STEP, axis=1, stride=1, stride_axis=0)
                sums.append(jnp.sum(skewed, axis=0, keepdims=True)[:, :tok])
            sums = jnp.concatenate(sums, axis=0).reshape(per // unit, unit, taps)
            lag[pl.ds((c * subs + s) * (per // unit), per // unit)] = sums

    def products(c):
        for s in range(subs):
            lanes = pl.ds(pl.multiple_of(c * width + s * LANES, LANES), LANES)
            first = pl.multiple_of((c * subs + s) * per, per)
            line = lines[pl.ds(first, per), :]
            band = jnp.concatenate(
                [
                    pltpu.roll(
                        jnp.broadcast_to(line[i : i + 1, :], (STEP, rows)), 1, axis=1, stride=1, stride_axis=0
                    ).astype(BF16)
                    for i in range(per)
                ],
                axis=0,
            )
            found = []
            for a in range(blocks):
                window = jnp.concatenate(
                    [ext_p[pl.ds(STEP * a, rows), lanes], ext_g[pl.ds(STEP * a, rows), lanes]], axis=1)
                res = jnp.dot(band, window, preferred_element_type=F32)
                out = res[0:STEP, :]
                for i in range(1, per):
                    out = jnp.where(owner == i, res[i * STEP : (i + 1) * STEP, :], out)
                found.append(out)
            whole = jnp.concatenate(found, axis=0)
            conv = whole[:, :LANES]
            back = whole[:, LANES:]
            coarse = back.astype(BF16)
            fine = (back - coarse.astype(F32)).astype(BF16)
            grad_prod = jnp.dot(flip2, jnp.concatenate([coarse, fine], axis=0), preferred_element_type=F32)
            mixed[:, lanes] = (q[:, lanes].astype(F32) * conv).astype(BF16)
            grad_q[:, lanes] = (g[:, lanes].astype(F32) * conv).astype(BF16)
            grad_k[:, lanes] = (grad_prod * v[:, lanes].astype(F32)).astype(BF16)
            grad_v[:, lanes] = (grad_prod * k[:, lanes].astype(F32)).astype(BF16)
    def store_all(c):
        for copy in stores(c):
            copy.start()

    @pl.loop(0, CHUNKS // 2)
    def _(h):
        for c in (2 * h, 2 * h + 1):
            sent(c)

            @pl.when(c + FLIGHT < CHUNKS)
            def _():
                send(c + FLIGHT)

            @pl.when(pos > 0)
            def _():
                to_next(c).wait_recv()

            @pl.when(pos < last)
            def _():
                to_previous(c).wait_recv()

        lag_sums(2 * h)
        lag_sums(2 * h + 1)
        products(h)
        store_all(h)

    @pl.loop(1, seq)
    def _(j):
        scatter(j).start()

    parts[0] = lag[pl.ds(pos * units, units)]

    @pl.loop(0, 2)
    def _(h):
        @pl.when(h == 1)
        def _():
            all_of(stage_recv, 0)
            mine[...] = jnp.sum(parts[...], axis=0)

            @pl.loop(1, dp)
            def _(j):
                exchange(j).start()

            shares[line_of] = mine[...]

        c = CHUNKS // 2 + h * (CHUNKS // 4)
        for i in range(CHUNKS // 4):
            products(c + i)
        for i in range(CHUNKS // 4):
            store_all(c + i)

    all_of(stage_recv, 1)
    total[...] = jnp.sum(shares[...], axis=0)

    @pl.loop(1, seq)
    def _(j):
        gather(j).start()

    gathered[pos] = total[...]

    all_of(stage_recv, 2)
    for stage in range(3):
        all_of(stage_send, stage)

    @pl.loop(0, CHUNKS)
    def _(c):
        for copy in stores(c):
            copy.wait()


def factor_kernel(scale, grads, basis, *refs):
    moved = tuple(zip(refs[:4], refs[4:8]))
    low_rank, basis_next = refs[8:10]
    held, sem_in, sem_out = refs[10:]
    piece = refs[0].shape[0] // PIECES

    def moves(inward):
        copies = []
        for i, (src, dst) in enumerate(moved):
            for p in range(PIECES):
                part = pl.ds(p * piece, piece)
                ends = (src.at[part], held.at[i, part]) if inward else (held.at[i, part], dst.at[part])
                copies.append(pltpu.make_async_copy(*ends, (sem_in if inward else sem_out).at[i, p]))
        return copies

    for copy in moves(True):
        copy.start()
    taps = grads.shape[1]
    flip_taps = flipped(taps, F32)
    basis_rev = jnp.dot(basis[...], flip_taps, precision=HIGHEST, preferred_element_type=F32)
    left = lax.dot_general(basis_rev, grads[...], NT, precision=HIGHEST, preferred_element_type=F32)
    rank = left.shape[0]
    index = lax.broadcasted_iota(jnp.int32, left.shape, 0)
    rest = left
    ortho = jnp.zeros_like(left)
    for i in range(rank):
        if i == 2:
            for arrived, leaving in zip(moves(True), moves(False)):
                arrived.wait()
                leaving.start()
        column = rest[i : i + 1, :]
        norm = jnp.sum(column * column, axis=1, keepdims=True) + 1e-06
        along = jnp.sum(left * column, axis=1, keepdims=True)
        ortho = jnp.where(index == i, column / jnp.sqrt(norm), ortho)
        rest = rest - (along / norm) * column
    right = jnp.dot(ortho, grads[...], precision=HIGHEST, preferred_element_type=F32) * scale
    right = jnp.dot(right, flip_taps, precision=HIGHEST, preferred_element_type=F32)
    basis_next[...] = right
    low_rank[...] = lax.dot_general(ortho, right, TN, precision=HIGHEST, preferred_element_type=F32)
    for copy in moves(False):
        copy.wait()


def on_device(query_gate, key_gate, value_feat, filters, grad_out, basis_prev):
    q, k, v, g = query_gate[0], key_gate[0], value_feat[0], grad_out[0]
    tok, channels = q.shape
    groups, taps = filters.shape
    rank = basis_prev.shape[1]
    scale = (lax.axis_size("dp") * lax.axis_size("seq") * tok * (channels // groups)) ** (-0.5)
    vmem = pl.BlockSpec(memory_space=pltpu.VMEM)
    anywhere = pl.BlockSpec(memory_space=pl.ANY)
    block = jax.ShapeDtypeStruct((tok, channels), BF16)
    held = pltpu.VMEM((tok, channels), BF16)
    padded = pltpu.VMEM((3 * tok - STEP, channels), BF16)
    per = LANES * groups // channels
    dp, seq = lax.axis_size("dp"), lax.axis_size("seq")
    unit = min(per, groups // seq)
    share = (groups // seq // unit, unit, taps)
    dma = pltpu.SemaphoreType.DMA
    *results, grads = pl.pallas_call(
        mixer_kernel,
        out_shape=(block,) * 4 + (jax.ShapeDtypeStruct((seq,) + share, F32),),
        in_specs=[anywhere] * 4 + [vmem],
        out_specs=[anywhere] * 4 + [vmem],
        scratch_shapes=[held] * 8 + [padded] * 2 + [
            pltpu.VMEM((groups, 2 * tok), F32),
            pltpu.VMEM((groups // unit, unit, taps), F32),
            pltpu.VMEM((seq,) + share, F32), pltpu.VMEM(share, F32),
            pltpu.VMEM((dp,) + share, F32), pltpu.VMEM(share, F32),
            dma((CHUNKS, 4)), dma((CHUNKS, 4)),
        ] + [dma((CHUNKS,))] * 4 + [dma((3,))] * 2,
        compiler_params=pltpu.CompilerParams(
            collective_id=0, has_side_effects=True, vmem_limit_bytes=56 * 2**20),
        name="mixer",
    )(q, k, v, g, filters)
    mixed, grad_q, grad_k, grad_v, low_rank, basis_next = pl.pallas_call(
        functools.partial(factor_kernel, scale),
        out_shape=(block,) * 4 + (
            jax.ShapeDtypeStruct((groups, taps), F32),
            jax.ShapeDtypeStruct((rank, taps), F32),
        ),
        in_specs=[vmem] * 2 + [anywhere] * 4,
        out_specs=[anywhere] * 4 + [vmem] * 2,
        scratch_shapes=[pltpu.VMEM((4, tok, channels), BF16), dma((4, PIECES)), dma((4, PIECES))],
        compiler_params=pltpu.CompilerParams(vmem_limit_bytes=56 * 2**20),
        name="factors",
    )(grads.reshape(groups, taps), basis_prev.T, *results)
    return (mixed[None], grad_q[None], grad_k[None], grad_v[None], low_rank, basis_next.T)


def solution(mesh):
    spec = P("dp", "seq", None)
    return jax.shard_map(
        on_device,
        mesh=mesh,
        in_specs=(spec, spec, spec, P(), spec, P()),
        out_specs=(spec, spec, spec, spec, P(), P()),
        check_vma=False,
    )
```

```python
import functools

import jax
import jax.numpy as jnp
from jax import lax
from jax.experimental import pallas as pl
from jax.experimental.pallas import tpu as pltpu
from jax.sharding import PartitionSpec as P

MESH = pl.DeviceIdType.MESH
HIGHEST = lax.Precision.HIGHEST
F32 = jnp.float32
BF16 = jnp.bfloat16
STEP = 32
LANES = 128
PIECES = 4
FLIGHT = 2
CHUNKS = 8
NT = (((1,), (1,)), ((), ()))
TN = (((0,), (0,)), ((), ()))


def flipped(size, dtype):
    rows = lax.broadcasted_iota(jnp.int32, (size, size), 0)
    cols = lax.broadcasted_iota(jnp.int32, (size, size), 1)
    return jnp.where(rows + cols == size - 1, 1.0, 0.0).astype(dtype)


def gated(left, right):
    return (left.astype(F32) * right.astype(F32)).astype(BF16)


def mixer_kernel(
    q_in, k_in, v_in, g_in, filters,
    mixed_out, grad_q_out, grad_k_out, grad_v_out, gathered,
    q, k, v, g, mixed, grad_q, grad_k, grad_v, ext_p, ext_g, lines, lag, parts, mine, shares, total,
    load, store, send_p, recv_p, send_g, recv_g, stage_send, stage_recv,
):
    dp, seq = lax.axis_size("dp"), lax.axis_size("seq")
    pos = lax.axis_index("seq")
    line_of = lax.axis_index("dp")
    last = seq - 1
    tok, channels = q.shape
    groups, taps = filters.shape
    group = channels // groups
    per = LANES // group
    width = channels // CHUNKS
    subs = width // LANES
    blocks = tok // STEP
    rows = 2 * tok
    units, unit = parts.shape[1:3]

    def chunk(c):
        return pl.ds(pl.multiple_of(c * width, width), width)

    def loads(c):
        return [
            pltpu.make_async_copy(src.at[:, chunk(c)], dst.at[:, chunk(c)], load.at[c, i])
            for i, (src, dst) in enumerate(((k_in, k), (v_in, v), (g_in, g), (q_in, q)))
        ]

    def stores(c):
        pairs = ((mixed, mixed_out), (grad_q, grad_q_out), (grad_k, grad_k_out), (grad_v, grad_v_out))
        return [
            pltpu.make_async_copy(src.at[:, chunk(c)], dst.at[:, chunk(c)], store.at[c, i])
            for i, (src, dst) in enumerate(pairs)
        ]

    def along_seq(j):
        return lax.rem(pos + j, seq)

    def along_dp(j):
        return lax.rem(line_of + j, dp)

    def to_next(c):
        return pltpu.make_async_remote_copy(
            src_ref=ext_p.at[pl.ds(tok, tok), chunk(c)], dst_ref=ext_p.at[pl.ds(0, tok), chunk(c)],
            send_sem=send_p.at[c], recv_sem=recv_p.at[c], device_id={"seq": pos + 1}, device_id_type=MESH)

    def to_previous(c):
        return pltpu.make_async_remote_copy(
            src_ref=ext_g.at[pl.ds(tok, tok), chunk(c)], dst_ref=ext_g.at[pl.ds(0, tok), chunk(c)],
            send_sem=send_g.at[c], recv_sem=recv_g.at[c], device_id={"seq": pos - 1}, device_id_type=MESH)

    def scatter(j):
        peer = along_seq(j)
        return pltpu.make_async_remote_copy(
            src_ref=lag.at[pl.ds(peer * units, units)], dst_ref=parts.at[j], send_sem=stage_send.at[0],
            recv_sem=stage_recv.at[0], device_id={"seq": peer}, device_id_type=MESH)

    def exchange(j):
        return pltpu.make_async_remote_copy(
            src_ref=mine, dst_ref=shares.at[line_of], send_sem=stage_send.at[1],
            recv_sem=stage_recv.at[1], device_id={"dp": along_dp(j)}, device_id_type=MESH)

    def gather(j):
        return pltpu.make_async_remote_copy(
            src_ref=total, dst_ref=gathered.at[pos], send_sem=stage_send.at[2],
            recv_sem=stage_recv.at[2], device_id={"seq": along_seq(j)}, device_id_type=MESH)

    def all_of(sems, stage):
        size = shares if stage == 1 else parts
        span = size.at[pl.ds(1, size.shape[0] - 1)]
        pltpu.make_async_copy(span, span, sems.at[stage]).wait()

    barrier = pltpu.get_barrier_semaphore()

    @pl.loop(0, CHUNKS)
    def _(c):
        for copy in loads(c):
            copy.start()

    @pl.loop(1, seq)
    def _(j):
        pl.semaphore_signal(barrier, inc=1, device_id={"seq": along_seq(j)}, device_id_type=MESH)

    @pl.loop(1, dp)
    def _(j):
        pl.semaphore_signal(barrier, inc=1, device_id={"dp": along_dp(j)}, device_id_type=MESH)

    flip = flipped(tok, BF16)
    flip2 = jnp.concatenate([flip, flip], axis=1)
    lines[:, :taps] = jnp.dot(filters[...], flip, preferred_element_type=F32)
    lines[:, taps:] = jnp.zeros((groups, rows - taps), F32)
    zeros = jnp.zeros((ext_p.shape[0] - rows, channels), BF16)
    ext_p[rows:, :] = zeros
    ext_g[rows:, :] = zeros

    @pl.when(pos == 0)
    def _():
        ext_p[0:tok, :] = jnp.zeros((tok, channels), BF16)

    @pl.when(pos == last)
    def _():
        ext_g[0:tok, :] = jnp.zeros((tok, channels), BF16)

    def gates(c):
        lanes = chunk(c)
        ext_p[pl.ds(tok, tok), lanes] = gated(k[:, lanes], v[:, lanes])
        ext_g[pl.ds(tok, tok), lanes] = jnp.dot(
            flip, gated(g[:, lanes], q[:, lanes]), preferred_element_type=F32).astype(BF16)

    def send(c):
        @pl.when(pos < last)
        def _():
            to_next(c).start()

        @pl.when(pos > 0)
        def _():
            to_previous(c).start()

    def sent(c):
        @pl.when(pos < last)
        def _():
            to_next(c).wait_send()

        @pl.when(pos > 0)
        def _():
            to_previous(c).wait_send()

    for low, high in ((0, 1), (1, FLIGHT), (FLIGHT, CHUNKS)):
        for c in range(low, high):
            for copy in loads(c):
                copy.wait()
        for c in range(low, high):
            gates(c)
        if low == 0:
            pl.semaphore_wait(barrier, seq + dp - 2)
        if low < FLIGHT:
            for c in range(low, high):
                send(c)

    owner = lax.broadcasted_iota(jnp.int32, (STEP, 2 * LANES), 1) % LANES // group

    def lag_sums(c):
        for s in range(subs):
            lanes = pl.ds(pl.multiple_of(c * width + s * LANES, LANES), LANES)
            cross = jnp.zeros((per * STEP, rows), F32)
            for one in range(0, blocks, 2):
                two = one + 1
                at_one = tok + STEP * (blocks - 1 - one)
                at_two = tok + STEP * (blocks - 1 - two)
                cot = jnp.concatenate(
                    [ext_g[pl.ds(at_one, STEP), lanes], ext_g[pl.ds(at_two, STEP), lanes]], axis=1)
                windows = jnp.concatenate(
                    [ext_p[pl.ds(STEP * one, rows), lanes], ext_p[pl.ds(STEP * two, rows), lanes]], axis=1)
                masked = jnp.concatenate(
                    [jnp.where(owner == i, cot, jnp.zeros_like(cot)) for i in range(per)], axis=0)
                cross = cross + lax.dot_general(masked, windows, NT, preferred_element_type=F32)
            sums = []
            for i in range(per):
                skewed = pltpu.roll(
                    cross[i * STEP : (i + 1) * STEP, :], rows - STEP, axis=1, stride=1, stride_axis=0)
                sums.append(jnp.sum(skewed, axis=0, keepdims=True)[:, :tok])
            sums = jnp.concatenate(sums, axis=0).reshape(per // unit, unit, taps)
            lag[pl.ds((c * subs + s) * (per // unit), per // unit)] = sums

    def products(low, blocks_of):
        for s in range(blocks_of):
            lanes = pl.ds(pl.multiple_of((low + s) * LANES, LANES), LANES)
            first = pl.multiple_of((low + s) * per, per)
            line = lines[pl.ds(first, per), :]
            band = jnp.concatenate(
                [
                    pltpu.roll(
                        jnp.broadcast_to(line[i : i + 1, :], (STEP, rows)), 1, axis=1, stride=1, stride_axis=0
                    ).astype(BF16)
                    for i in range(per)
                ],
                axis=0,
            )
            found = []
            for a in range(blocks):
                window = jnp.concatenate(
                    [ext_p[pl.ds(STEP * a, rows), lanes], ext_g[pl.ds(STEP * a, rows), lanes]], axis=1)
                res = jnp.dot(band, window, preferred_element_type=F32)
                out = res[0:STEP, :]
                for i in range(1, per):
                    out = jnp.where(owner == i, res[i * STEP : (i + 1) * STEP, :], out)
                found.append(out)
            whole = jnp.concatenate(found, axis=0)
            conv = whole[:, :LANES]
            back = whole[:, LANES:]
            coarse = back.astype(BF16)
            fine = (back - coarse.astype(F32)).astype(BF16)
            grad_prod = jnp.dot(flip2, jnp.concatenate([coarse, fine], axis=0), preferred_element_type=F32)
            mixed[:, lanes] = (q[:, lanes].astype(F32) * conv).astype(BF16)
            grad_q[:, lanes] = (g[:, lanes].astype(F32) * conv).astype(BF16)
            grad_k[:, lanes] = (grad_prod * v[:, lanes].astype(F32)).astype(BF16)
            grad_v[:, lanes] = (grad_prod * k[:, lanes].astype(F32)).astype(BF16)
    def store_all(c):
        for copy in stores(c):
            copy.start()

    @pl.loop(0, CHUNKS // 2)
    def _(h):
        for c in (2 * h, 2 * h + 1):
            sent(c)

            @pl.when(c + FLIGHT < CHUNKS)
            def _():
                send(c + FLIGHT)

            @pl.when(pos > 0)
            def _():
                to_next(c).wait_recv()

            @pl.when(pos < last)
            def _():
                to_previous(c).wait_recv()

        lag_sums(2 * h)
        lag_sums(2 * h + 1)
        products(h * subs, subs)
        store_all(h)

    @pl.loop(1, seq)
    def _(j):
        scatter(j).start()

    parts[0] = lag[pl.ds(pos * units, units)]

    left_over = (CHUNKS - CHUNKS // 2) * subs
    third = left_over // 3
    start = (CHUNKS // 2) * subs
    products(start, left_over - 2 * third)
    all_of(stage_recv, 0)
    mine[...] = jnp.sum(parts[...], axis=0)

    @pl.loop(1, dp)
    def _(j):
        exchange(j).start()

    shares[line_of] = mine[...]
    store_all(CHUNKS // 2)
    start += left_over - 2 * third
    products(start, third)
    all_of(stage_recv, 1)
    total[...] = jnp.sum(shares[...], axis=0)

    @pl.loop(1, seq)
    def _(j):
        gather(j).start()

    gathered[pos] = total[...]
    products(start + third, third)
    for c in range(CHUNKS // 2 + 1, CHUNKS):
        store_all(c)

    all_of(stage_recv, 2)
    for stage in range(3):
        all_of(stage_send, stage)

    @pl.loop(0, CHUNKS)
    def _(c):
        for copy in stores(c):
            copy.wait()


def factor_kernel(scale, grads, basis, *refs):
    moved = tuple(zip(refs[:4], refs[4:8]))
    low_rank, basis_next = refs[8:10]
    held, sem_in, sem_out = refs[10:]
    piece = refs[0].shape[0] // PIECES

    def moves(inward):
        copies = []
        for i, (src, dst) in enumerate(moved):
            for p in range(PIECES):
                part = pl.ds(p * piece, piece)
                ends = (src.at[part], held.at[i, part]) if inward else (held.at[i, part], dst.at[part])
                copies.append(pltpu.make_async_copy(*ends, (sem_in if inward else sem_out).at[i, p]))
        return copies

    for copy in moves(True):
        copy.start()
    taps = grads.shape[1]
    flip_taps = flipped(taps, F32)
    basis_rev = jnp.dot(basis[...], flip_taps, precision=HIGHEST, preferred_element_type=F32)
    left = lax.dot_general(basis_rev, grads[...], NT, precision=HIGHEST, preferred_element_type=F32)
    rank = left.shape[0]
    index = lax.broadcasted_iota(jnp.int32, left.shape, 0)
    rest = left
    ortho = jnp.zeros_like(left)
    for i in range(rank):
        if i == 2:
            for arrived, leaving in zip(moves(True), moves(False)):
                arrived.wait()
                leaving.start()
        column = rest[i : i + 1, :]
        norm = jnp.sum(column * column, axis=1, keepdims=True) + 1e-06
        along = jnp.sum(left * column, axis=1, keepdims=True)
        ortho = jnp.where(index == i, column / jnp.sqrt(norm), ortho)
        rest = rest - (along / norm) * column
    right = jnp.dot(ortho, grads[...], precision=HIGHEST, preferred_element_type=F32) * scale
    right = jnp.dot(right, flip_taps, precision=HIGHEST, preferred_element_type=F32)
    basis_next[...] = right
    low_rank[...] = lax.dot_general(ortho, right, TN, precision=HIGHEST, preferred_element_type=F32)
    for copy in moves(False):
        copy.wait()


def on_device(query_gate, key_gate, value_feat, filters, grad_out, basis_prev):
    q, k, v, g = query_gate[0], key_gate[0], value_feat[0], grad_out[0]
    tok, channels = q.shape
    groups, taps = filters.shape
    rank = basis_prev.shape[1]
    scale = (lax.axis_size("dp") * lax.axis_size("seq") * tok * (channels // groups)) ** (-0.5)
    vmem = pl.BlockSpec(memory_space=pltpu.VMEM)
    anywhere = pl.BlockSpec(memory_space=pl.ANY)
    block = jax.ShapeDtypeStruct((tok, channels), BF16)
    held = pltpu.VMEM((tok, channels), BF16)
    padded = pltpu.VMEM((3 * tok - STEP, channels), BF16)
    per = LANES * groups // channels
    dp, seq = lax.axis_size("dp"), lax.axis_size("seq")
    unit = min(per, groups // seq)
    share = (groups // seq // unit, unit, taps)
    dma = pltpu.SemaphoreType.DMA
    *results, grads = pl.pallas_call(
        mixer_kernel,
        out_shape=(block,) * 4 + (jax.ShapeDtypeStruct((seq,) + share, F32),),
        in_specs=[anywhere] * 4 + [vmem],
        out_specs=[anywhere] * 4 + [vmem],
        scratch_shapes=[held] * 8 + [padded] * 2 + [
            pltpu.VMEM((groups, 2 * tok), F32),
            pltpu.VMEM((groups // unit, unit, taps), F32),
            pltpu.VMEM((seq,) + share, F32), pltpu.VMEM(share, F32),
            pltpu.VMEM((dp,) + share, F32), pltpu.VMEM(share, F32),
            dma((CHUNKS, 4)), dma((CHUNKS, 4)),
        ] + [dma((CHUNKS,))] * 4 + [dma((3,))] * 2,
        compiler_params=pltpu.CompilerParams(
            collective_id=0, has_side_effects=True, vmem_limit_bytes=56 * 2**20),
        name="mixer",
    )(q, k, v, g, filters)
    mixed, grad_q, grad_k, grad_v, low_rank, basis_next = pl.pallas_call(
        functools.partial(factor_kernel, scale),
        out_shape=(block,) * 4 + (
            jax.ShapeDtypeStruct((groups, taps), F32),
            jax.ShapeDtypeStruct((rank, taps), F32),
        ),
        in_specs=[vmem] * 2 + [anywhere] * 4,
        out_specs=[anywhere] * 4 + [vmem] * 2,
        scratch_shapes=[pltpu.VMEM((4, tok, channels), BF16), dma((4, PIECES)), dma((4, PIECES))],
        compiler_params=pltpu.CompilerParams(vmem_limit_bytes=56 * 2**20),
        name="factors",
    )(grads.reshape(groups, taps), basis_prev.T, *results)
    return (mixed[None], grad_q[None], grad_k[None], grad_v[None], low_rank, basis_next.T)


def solution(mesh):
    spec = P("dp", "seq", None)
    return jax.shard_map(
        on_device,
        mesh=mesh,
        in_specs=(spec, spec, spec, P(), spec, P()),
        out_specs=(spec, spec, spec, spec, P(), P()),
        check_vma=False,
    )
```

```python
import functools

import jax
import jax.numpy as jnp
from jax import lax
from jax.experimental import pallas as pl
from jax.experimental.pallas import tpu as pltpu
from jax.sharding import PartitionSpec as P

MESH = pl.DeviceIdType.MESH
HIGHEST = lax.Precision.HIGHEST
F32 = jnp.float32
BF16 = jnp.bfloat16
STEP = 32
LANES = 128
PIECES = 4
CHUNKS = 8
NT = (((1,), (1,)), ((), ()))
TN = (((0,), (0,)), ((), ()))


def flipped(size, dtype):
    rows = lax.broadcasted_iota(jnp.int32, (size, size), 0)
    cols = lax.broadcasted_iota(jnp.int32, (size, size), 1)
    return jnp.where(rows + cols == size - 1, 1.0, 0.0).astype(dtype)


def gated(left, right):
    return (left.astype(F32) * right.astype(F32)).astype(BF16)


def mixer_kernel(
    q_in, k_in, v_in, g_in, filters,
    mixed_out, grad_q_out, grad_k_out, grad_v_out, gathered,
    q, k, v, g, mixed, grad_q, grad_k, grad_v, ext_p, ext_g, lines, lag, parts, mine, shares, total,
    load, store, send_p, recv_p, send_g, recv_g, stage_send, stage_recv,
):
    dp, seq = lax.axis_size("dp"), lax.axis_size("seq")
    pos = lax.axis_index("seq")
    line_of = lax.axis_index("dp")
    last = seq - 1
    tok, channels = q.shape
    groups, taps = filters.shape
    group = channels // groups
    per = LANES // group
    width = channels // CHUNKS
    subs = width // LANES
    blocks = tok // STEP
    rows = 2 * tok
    units, unit = parts.shape[1:3]

    def chunk(c):
        return pl.ds(pl.multiple_of(c * width, width), width)

    def loads(c):
        return [
            pltpu.make_async_copy(src.at[:, chunk(c)], dst.at[:, chunk(c)], load.at[c, i])
            for i, (src, dst) in enumerate(((k_in, k), (v_in, v), (g_in, g), (q_in, q)))
        ]

    def stores(c):
        pairs = ((mixed, mixed_out), (grad_q, grad_q_out), (grad_k, grad_k_out), (grad_v, grad_v_out))
        return [
            pltpu.make_async_copy(src.at[:, chunk(c)], dst.at[:, chunk(c)], store.at[c, i])
            for i, (src, dst) in enumerate(pairs)
        ]

    def along_seq(j):
        return lax.rem(pos + j, seq)

    def along_dp(j):
        return lax.rem(line_of + j, dp)

    def to_next(c):
        return pltpu.make_async_remote_copy(
            src_ref=ext_p.at[pl.ds(tok, tok), chunk(c)], dst_ref=ext_p.at[pl.ds(0, tok), chunk(c)],
            send_sem=send_p.at[c], recv_sem=recv_p.at[c], device_id={"seq": pos + 1}, device_id_type=MESH)

    def to_previous(c):
        return pltpu.make_async_remote_copy(
            src_ref=ext_g.at[pl.ds(tok, tok), chunk(c)], dst_ref=ext_g.at[pl.ds(0, tok), chunk(c)],
            send_sem=send_g.at[c], recv_sem=recv_g.at[c], device_id={"seq": pos - 1}, device_id_type=MESH)

    def scatter(j):
        peer = along_seq(j)
        return pltpu.make_async_remote_copy(
            src_ref=lag.at[pl.ds(peer * units, units)], dst_ref=parts.at[j], send_sem=stage_send.at[0],
            recv_sem=stage_recv.at[0], device_id={"seq": peer}, device_id_type=MESH)

    def exchange(j):
        return pltpu.make_async_remote_copy(
            src_ref=mine, dst_ref=shares.at[line_of], send_sem=stage_send.at[1],
            recv_sem=stage_recv.at[1], device_id={"dp": along_dp(j)}, device_id_type=MESH)

    def gather(j):
        return pltpu.make_async_remote_copy(
            src_ref=total, dst_ref=gathered.at[pos], send_sem=stage_send.at[2],
            recv_sem=stage_recv.at[2], device_id={"seq": along_seq(j)}, device_id_type=MESH)

    def all_of(sems, stage):
        size = shares if stage == 1 else parts
        span = size.at[pl.ds(1, size.shape[0] - 1)]
        pltpu.make_async_copy(span, span, sems.at[stage]).wait()

    barrier = pltpu.get_barrier_semaphore()

    @pl.loop(0, CHUNKS)
    def _(c):
        for copy in loads(c):
            copy.start()

    @pl.loop(1, seq)
    def _(j):
        pl.semaphore_signal(barrier, inc=1, device_id={"seq": along_seq(j)}, device_id_type=MESH)

    @pl.loop(1, dp)
    def _(j):
        pl.semaphore_signal(barrier, inc=1, device_id={"dp": along_dp(j)}, device_id_type=MESH)

    flip = flipped(tok, BF16)
    flip2 = jnp.concatenate([flip, flip], axis=1)
    lines[:, :taps] = jnp.dot(filters[...], flip, preferred_element_type=F32)
    lines[:, taps:] = jnp.zeros((groups, rows - taps), F32)
    zeros = jnp.zeros((ext_p.shape[0] - rows, channels), BF16)
    ext_p[rows:, :] = zeros
    ext_g[rows:, :] = zeros

    @pl.when(pos == 0)
    def _():
        ext_p[0:tok, :] = jnp.zeros((tok, channels), BF16)

    @pl.when(pos == last)
    def _():
        ext_g[0:tok, :] = jnp.zeros((tok, channels), BF16)

    def gates(c):
        lanes = chunk(c)
        ext_p[pl.ds(tok, tok), lanes] = gated(k[:, lanes], v[:, lanes])
        ext_g[pl.ds(tok, tok), lanes] = jnp.dot(
            flip, gated(g[:, lanes], q[:, lanes]), preferred_element_type=F32).astype(BF16)

    def send(c):
        @pl.when(pos < last)
        def _():
            to_next(c).start()

        @pl.when(pos > 0)
        def _():
            to_previous(c).start()

    def sent(c):
        @pl.when(pos < last)
        def _():
            to_next(c).wait_send()

        @pl.when(pos > 0)
        def _():
            to_previous(c).wait_send()

    for low, high in ((0, 1), (1, 3), (3, CHUNKS)):
        for c in range(low, high):
            for copy in loads(c):
                copy.wait()
        for c in range(low, high):
            gates(c)
        if low == 0:
            pl.semaphore_wait(barrier, seq + dp - 2)
        for c in range(low, high):
            send(c)

    owner = lax.broadcasted_iota(jnp.int32, (STEP, 2 * LANES), 1) % LANES // group

    def lag_sums(c):
        for s in range(subs):
            lanes = pl.ds(pl.multiple_of(c * width + s * LANES, LANES), LANES)
            cross = jnp.zeros((per * STEP, rows), F32)
            for one in range(0, blocks, 2):
                two = one + 1
                at_one = tok + STEP * (blocks - 1 - one)
                at_two = tok + STEP * (blocks - 1 - two)
                cot = jnp.concatenate(
                    [ext_g[pl.ds(at_one, STEP), lanes], ext_g[pl.ds(at_two, STEP), lanes]], axis=1)
                windows = jnp.concatenate(
                    [ext_p[pl.ds(STEP * one, rows), lanes], ext_p[pl.ds(STEP * two, rows), lanes]], axis=1)
                masked = jnp.concatenate(
                    [jnp.where(owner == i, cot, jnp.zeros_like(cot)) for i in range(per)], axis=0)
                cross = cross + lax.dot_general(masked, windows, NT, preferred_element_type=F32)
            sums = []
            for i in range(per):
                skewed = pltpu.roll(
                    cross[i * STEP : (i + 1) * STEP, :], rows - STEP, axis=1, stride=1, stride_axis=0)
                sums.append(jnp.sum(skewed, axis=0, keepdims=True)[:, :tok])
            sums = jnp.concatenate(sums, axis=0).reshape(per // unit, unit, taps)
            lag[pl.ds((c * subs + s) * (per // unit), per // unit)] = sums

    def products(low, blocks_of):
        for s in range(blocks_of):
            lanes = pl.ds(pl.multiple_of((low + s) * LANES, LANES), LANES)
            first = pl.multiple_of((low + s) * per, per)
            line = lines[pl.ds(first, per), :]
            band = jnp.concatenate(
                [
                    pltpu.roll(
                        jnp.broadcast_to(line[i : i + 1, :], (STEP, rows)), 1, axis=1, stride=1, stride_axis=0
                    ).astype(BF16)
                    for i in range(per)
                ],
                axis=0,
            )
            found = []
            for a in range(blocks):
                window = jnp.concatenate(
                    [ext_p[pl.ds(STEP * a, rows), lanes], ext_g[pl.ds(STEP * a, rows), lanes]], axis=1)
                res = jnp.dot(band, window, preferred_element_type=F32)
                out = res[0:STEP, :]
                for i in range(1, per):
                    out = jnp.where(owner == i, res[i * STEP : (i + 1) * STEP, :], out)
                found.append(out)
            whole = jnp.concatenate(found, axis=0)
            conv = whole[:, :LANES]
            back = whole[:, LANES:]
            coarse = back.astype(BF16)
            fine = (back - coarse.astype(F32)).astype(BF16)
            grad_prod = jnp.dot(flip2, jnp.concatenate([coarse, fine], axis=0), preferred_element_type=F32)
            mixed[:, lanes] = (q[:, lanes].astype(F32) * conv).astype(BF16)
            grad_q[:, lanes] = (g[:, lanes].astype(F32) * conv).astype(BF16)
            grad_k[:, lanes] = (grad_prod * v[:, lanes].astype(F32)).astype(BF16)
            grad_v[:, lanes] = (grad_prod * k[:, lanes].astype(F32)).astype(BF16)
    def store_all(c):
        for copy in stores(c):
            copy.start()

    @pl.loop(0, CHUNKS // 2)
    def _(h):
        for c in (2 * h, 2 * h + 1):
            @pl.when(pos > 0)
            def _():
                to_next(c).wait_recv()

            @pl.when(pos < last)
            def _():
                to_previous(c).wait_recv()

        lag_sums(2 * h)
        lag_sums(2 * h + 1)
        products(h * subs, subs)
        store_all(h)

    @pl.loop(1, seq)
    def _(j):
        scatter(j).start()

    parts[0] = lag[pl.ds(pos * units, units)]

    left_over = (CHUNKS - CHUNKS // 2) * subs
    third = left_over // 3
    start = (CHUNKS // 2) * subs
    products(start, left_over - 2 * third)
    all_of(stage_recv, 0)
    mine[...] = jnp.sum(parts[...], axis=0)

    @pl.loop(1, dp)
    def _(j):
        exchange(j).start()

    shares[line_of] = mine[...]
    store_all(CHUNKS // 2)
    start += left_over - 2 * third
    products(start, third)
    all_of(stage_recv, 1)
    total[...] = jnp.sum(shares[...], axis=0)

    @pl.loop(1, seq)
    def _(j):
        gather(j).start()

    gathered[pos] = total[...]
    products(start + third, third)
    for c in range(CHUNKS // 2 + 1, CHUNKS):
        store_all(c)

    all_of(stage_recv, 2)
    for stage in range(3):
        all_of(stage_send, stage)

    @pl.loop(0, CHUNKS)
    def _(c):
        sent(c)
        for copy in stores(c):
            copy.wait()


def factor_kernel(scale, grads, basis, *refs):
    moved = tuple(zip(refs[:4], refs[4:8]))
    low_rank, basis_next = refs[8:10]
    held, sem_in, sem_out = refs[10:]
    piece = refs[0].shape[0] // PIECES

    def moves(inward):
        copies = []
        for i, (src, dst) in enumerate(moved):
            for p in range(PIECES):
                part = pl.ds(p * piece, piece)
                ends = (src.at[part], held.at[i, part]) if inward else (held.at[i, part], dst.at[part])
                copies.append(pltpu.make_async_copy(*ends, (sem_in if inward else sem_out).at[i, p]))
        return copies

    for copy in moves(True):
        copy.start()
    taps = grads.shape[1]
    flip_taps = flipped(taps, F32)
    basis_rev = jnp.dot(basis[...], flip_taps, precision=HIGHEST, preferred_element_type=F32)
    left = lax.dot_general(basis_rev, grads[...], NT, precision=HIGHEST, preferred_element_type=F32)
    rank = left.shape[0]
    index = lax.broadcasted_iota(jnp.int32, left.shape, 0)
    rest = left
    ortho = jnp.zeros_like(left)
    for i in range(rank):
        if i == 2:
            for arrived, leaving in zip(moves(True), moves(False)):
                arrived.wait()
                leaving.start()
        column = rest[i : i + 1, :]
        norm = jnp.sum(column * column, axis=1, keepdims=True) + 1e-06
        along = jnp.sum(left * column, axis=1, keepdims=True)
        ortho = jnp.where(index == i, column / jnp.sqrt(norm), ortho)
        rest = rest - (along / norm) * column
    right = jnp.dot(ortho, grads[...], precision=HIGHEST, preferred_element_type=F32) * scale
    right = jnp.dot(right, flip_taps, precision=HIGHEST, preferred_element_type=F32)
    basis_next[...] = right
    low_rank[...] = lax.dot_general(ortho, right, TN, precision=HIGHEST, preferred_element_type=F32)
    for copy in moves(False):
        copy.wait()


def on_device(query_gate, key_gate, value_feat, filters, grad_out, basis_prev):
    q, k, v, g = query_gate[0], key_gate[0], value_feat[0], grad_out[0]
    tok, channels = q.shape
    groups, taps = filters.shape
    rank = basis_prev.shape[1]
    scale = (lax.axis_size("dp") * lax.axis_size("seq") * tok * (channels // groups)) ** (-0.5)
    vmem = pl.BlockSpec(memory_space=pltpu.VMEM)
    anywhere = pl.BlockSpec(memory_space=pl.ANY)
    block = jax.ShapeDtypeStruct((tok, channels), BF16)
    held = pltpu.VMEM((tok, channels), BF16)
    padded = pltpu.VMEM((3 * tok - STEP, channels), BF16)
    per = LANES * groups // channels
    dp, seq = lax.axis_size("dp"), lax.axis_size("seq")
    unit = min(per, groups // seq)
    share = (groups // seq // unit, unit, taps)
    dma = pltpu.SemaphoreType.DMA
    *results, grads = pl.pallas_call(
        mixer_kernel,
        out_shape=(block,) * 4 + (jax.ShapeDtypeStruct((seq,) + share, F32),),
        in_specs=[anywhere] * 4 + [vmem],
        out_specs=[anywhere] * 4 + [vmem],
        scratch_shapes=[held] * 8 + [padded] * 2 + [
            pltpu.VMEM((groups, 2 * tok), F32),
            pltpu.VMEM((groups // unit, unit, taps), F32),
            pltpu.VMEM((seq,) + share, F32), pltpu.VMEM(share, F32),
            pltpu.VMEM((dp,) + share, F32), pltpu.VMEM(share, F32),
            dma((CHUNKS, 4)), dma((CHUNKS, 4)),
        ] + [dma((CHUNKS,))] * 4 + [dma((3,))] * 2,
        compiler_params=pltpu.CompilerParams(
            collective_id=0, has_side_effects=True, vmem_limit_bytes=56 * 2**20),
        name="mixer",
    )(q, k, v, g, filters)
    mixed, grad_q, grad_k, grad_v, low_rank, basis_next = pl.pallas_call(
        functools.partial(factor_kernel, scale),
        out_shape=(block,) * 4 + (
            jax.ShapeDtypeStruct((groups, taps), F32),
            jax.ShapeDtypeStruct((rank, taps), F32),
        ),
        in_specs=[vmem] * 2 + [anywhere] * 4,
        out_specs=[anywhere] * 4 + [vmem] * 2,
        scratch_shapes=[pltpu.VMEM((4, tok, channels), BF16), dma((4, PIECES)), dma((4, PIECES))],
        compiler_params=pltpu.CompilerParams(vmem_limit_bytes=56 * 2**20),
        name="factors",
    )(grads.reshape(groups, taps), basis_prev.T, *results)
    return (mixed[None], grad_q[None], grad_k[None], grad_v[None], low_rank, basis_next.T)


def solution(mesh):
    spec = P("dp", "seq", None)
    return jax.shard_map(
        on_device,
        mesh=mesh,
        in_specs=(spec, spec, spec, P(), spec, P()),
        out_specs=(spec, spec, spec, spec, P(), P()),
        check_vma=False,
    )
```
